32 devices in a mesh: wide: 8 (over z, x), narrow: 4 (over y, core).
Axes of the slice: x: 2, y: 2, z: 4, core: 2. Of those that a mesh axis runs over, the one named last changes fastest.
Arguments:
- links: float32 [4, 4, 16, 4, 3072], P(None, None, 'wide', 'narrow'), may hold values from -1 to 1, as said below
- gauge: float32 [4, 16, 4, 3072], P(None, 'wide', 'narrow'), may hold values from -1 to 1, as said below
Outputs:
- spectrum: float32 [2, 12, 64, 48, 64], P(None, None, 'wide', 'narrow')
- fixed_gauge: float32 [4, 16, 4, 3072], P(None, 'wide', 'narrow')
The draws below stay inside these ranges and needn't reach their ends.
Inputs may be any that keep to these rules, and one draw needn't show every extreme that they name: `links`: the four quaternion components of every link form a unit vector, so each link is an SU(2) matrix. `gauge`: the four quaternion components at every site form a unit vector.
All inputs are finite; a program needn't handle non-finite values.
Results may differ from the reference program's by a relative error of at most 0.00015.
Values sent between devices are 32-bit elements; how exact they have to be, the bound alone decides.
A program may use at most 64 MiB of HBM per device.

```python
import math
import jax
import jax.numpy as jnp
from jax import lax

LY = 64
LT = 48
HALF_SWEEPS = 2
NX = 16
NZ = 4


def unit_quaternions(key, shape, lower, spread):
    key_one, key_two, key_three = jax.random.split(key, 3)
    first = jax.random.uniform(key_one, shape, jnp.float32, lower, 1.0)
    second = jax.random.uniform(key_two, shape, jnp.float32, 0.0, 1.0)
    third = jax.random.uniform(key_three, shape, jnp.float32, -spread, spread)
    outer = jnp.sqrt(1.0 - first)
    inner = jnp.sqrt(first)
    turn = 2.0 * math.pi
    return jnp.stack([inner * jnp.cos(turn * third), outer * jnp.sin(turn * second), outer * jnp.cos(turn * second), inner * jnp.sin(turn * third)])


def draw_links(key, part):
    key = jax.random.fold_in(key, 11)
    return unit_quaternions(key, (4, NX, NZ, LY * LT), 0.0, 0.5)


def draw_gauge(key, part):
    key = jax.random.fold_in(key, 23)
    return unit_quaternions(key, (NX, NZ, LY * LT), 0.0, 0.5)


def setup_inputs(seed: int = 0) -> dict:
    keys = jax.random.split(jax.random.key(seed), 3)
    links = draw_links(jax.random.fold_in(keys[2], 71), 0)
    gauge = draw_gauge(jax.random.fold_in(keys[2], 71), 0)
    return {"links": links, "gauge": gauge}


OMEGA = 1.7

def quat_product(first_quat, second_quat):
    scalar = first_quat[0] * second_quat[0] - first_quat[1] * second_quat[1] - first_quat[2] * second_quat[2] - first_quat[3] * second_quat[3]
    vector_one = first_quat[0] * second_quat[1] + second_quat[0] * first_quat[1] - (first_quat[2] * second_quat[3] - first_quat[3] * second_quat[2])
    vector_two = first_quat[0] * second_quat[2] + second_quat[0] * first_quat[2] - (first_quat[3] * second_quat[1] - first_quat[1] * second_quat[3])
    vector_three = first_quat[0] * second_quat[3] + second_quat[0] * first_quat[3] - (first_quat[1] * second_quat[2] - first_quat[2] * second_quat[1])
    return jnp.stack([scalar, vector_one, vector_two, vector_three])

def quat_conj(quaternion):
    return jnp.concatenate([quaternion[:1], -quaternion[1:]], axis=0)

def relax_sites(field, kernel_sum):
    kernel_norm = jnp.sqrt(lax.optimization_barrier(jnp.sum(kernel_sum * kernel_sum, axis=0)))
    rotated = OMEGA * quat_product(quat_conj(kernel_sum), quat_conj(field))
    relaxed = jnp.concatenate([rotated[:1] + (1.0 - OMEGA) * kernel_norm[None], rotated[1:]], axis=0)
    relaxed_norm = jnp.sqrt(lax.optimization_barrier(jnp.sum(relaxed * relaxed, axis=0)))
    return quat_product(relaxed, field) / jnp.maximum(relaxed_norm, 1.0)[None]

def site_parity(coord_x, coord_z):
    rows_y = jnp.arange(LY, dtype=jnp.int32)
    rows_t = jnp.arange(LT, dtype=jnp.int32)
    return (coord_x[:, None, None, None] + coord_z[None, :, None, None] + rows_y[None, None, :, None] + rows_t[None, None, None, :]) % 2

def reference(links, gauge):
    link = links.reshape((4, 4, NX, NZ, LY, LT))
    field = gauge.reshape((4, NX, NZ, LY, LT))
    axis_of = (1, 3, 2, 4)
    parity = site_parity(jnp.arange(NX, dtype=jnp.int32), jnp.arange(NZ, dtype=jnp.int32))
    behind_links = [jnp.roll(link[:, direction], 1, axis=axis_of[direction]) for direction in range(4)]
    for half_sweep in range(HALF_SWEEPS):
        update_side = half_sweep % 2
        kernel_sum = jnp.zeros(field.shape, jnp.float32)
        for direction in range(4):
            ahead = jnp.roll(field, -1, axis=axis_of[direction])
            behind = jnp.roll(field, 1, axis=axis_of[direction])
            kernel_sum = kernel_sum + quat_product(link[:, direction], quat_conj(ahead)) + quat_product(quat_conj(behind_links[direction]), quat_conj(behind))
        field = jnp.where((parity == update_side)[None], relax_sites(field, kernel_sum), field)
    pieces = []
    for direction in range(4):
        ahead = jnp.roll(field, -1, axis=axis_of[direction])
        transformed = quat_product(quat_product(field, link[:, direction]), quat_conj(ahead))
        pieces.append(transformed[1:])
    potential = jnp.stack(pieces, axis=1).reshape((12, NX, NZ, LY, LT))
    scale = float(NX * NZ * LY * LT) ** (-0.5)

    def transform(component):
        result = jnp.fft.fftn(component) * scale
        return jnp.stack([jnp.real(result), jnp.imag(result)]).astype(jnp.float32)
    spectra = lax.map(transform, potential)
    spectra = jnp.transpose(spectra, (1, 0, 4, 5, 2, 3)).reshape((2, 12, LY, LT, NX * NZ))
    return (spectra, field.reshape((4, NX, NZ, LY * LT)))
```

```python
import math

import jax
import jax.numpy as jnp
import numpy as np
from jax import lax
from jax.experimental import pallas as pl
from jax.experimental.pallas import tpu as pltpu
from jax.sharding import PartitionSpec as P

LY = 64
LT = 48
HALF_SWEEPS = 2


OMEGA = 1.7


def from_behind(value, axis, steps):
    count = lax.axis_size(axis)
    pairs = [(source, (source + steps) % count) for source in range(count)]
    return lax.ppermute(value, axis, pairs)


def padded_2(block, sides, width):
    for axis, dim in sides:
        count = lax.axis_size(axis)
        forward = [(i, i + 1) for i in range(count - 1)]
        forward.append((count - 1, 0))
        backward = [(target, source) for source, target in forward]
        low = lax.ppermute(
            lax.slice_in_dim(block, block.shape[dim] - width, None, axis=dim), axis, forward
        )
        high = lax.ppermute(lax.slice_in_dim(block, 0, width, axis=dim), axis, backward)
        block = jnp.concatenate([low, block, high], axis=dim)
    return block


def quat_product(first_quat, second_quat):
    scalar = (
        first_quat[0] * second_quat[0]
        - first_quat[1] * second_quat[1]
        - first_quat[2] * second_quat[2]
        - first_quat[3] * second_quat[3]
    )
    vector_one = (
        first_quat[0] * second_quat[1]
        + second_quat[0] * first_quat[1]
        - (first_quat[2] * second_quat[3] - first_quat[3] * second_quat[2])
    )
    vector_two = (
        first_quat[0] * second_quat[2]
        + second_quat[0] * first_quat[2]
        - (first_quat[3] * second_quat[1] - first_quat[1] * second_quat[3])
    )
    vector_three = (
        first_quat[0] * second_quat[3]
        + second_quat[0] * first_quat[3]
        - (first_quat[1] * second_quat[2] - first_quat[2] * second_quat[1])
    )
    return jnp.stack([scalar, vector_one, vector_two, vector_three])


def quat_conj(quaternion):
    return jnp.concatenate([quaternion[:1], -quaternion[1:]], axis=0)


def relax_sites(field, kernel_sum):
    kernel_norm = jnp.sqrt(jnp.sum(kernel_sum * kernel_sum, axis=0))
    rotated = OMEGA * quat_product(quat_conj(kernel_sum), quat_conj(field))
    relaxed = jnp.concatenate(
        [rotated[:1] + (1.0 - OMEGA) * kernel_norm[None], rotated[1:]], axis=0
    )
    relaxed_norm = jnp.sqrt(jnp.sum(relaxed * relaxed, axis=0))
    return quat_product(relaxed, field) / jnp.maximum(relaxed_norm, 1.0)[None]


def site_parity(coord_x, coord_z):
    rows_y = jnp.arange(LY, dtype=jnp.int32)
    rows_t = jnp.arange(LT, dtype=jnp.int32)
    return (
        coord_x[:, None, None, None]
        + coord_z[None, :, None, None]
        + rows_y[None, None, :, None]
        + rows_t[None, None, None, :]
    ) % 2


def fourier_tables(length):
    indices = jnp.arange(length, dtype=jnp.int32)
    phases = indices[:, None] * indices[None, :] % length
    angles = phases.astype(jnp.float32) * (2.0 * math.pi / length)
    return (jnp.cos(angles), jnp.sin(angles))


def along_axis(spectrum, axis_number):
    cosine, sine_part = fourier_tables(spectrum.shape[axis_number])
    moved_last = jnp.moveaxis(spectrum, axis_number, -1)
    cos_term = jnp.matmul(moved_last, cosine, precision=lax.Precision.HIGHEST)
    sin_term = jnp.matmul(moved_last, sine_part, precision=lax.Precision.HIGHEST)
    rotated = jnp.stack([cos_term[0] + sin_term[1], cos_term[1] - sin_term[0]])
    return jnp.moveaxis(rotated, -1, axis_number)


def along_x(spectrum):
    return along_axis(spectrum, 2)


def along_z(spectrum):
    return along_axis(spectrum, 3)


def body(links, gauge):
    slab_x = gauge.shape[1]
    slab_z = gauge.shape[2]
    count_wide = lax.axis_size("wide")
    count_narrow = lax.axis_size("narrow")
    coord_x = lax.axis_index("wide") * slab_x + jnp.arange(slab_x, dtype=jnp.int32)
    coord_z = lax.axis_index("narrow") * slab_z + jnp.arange(slab_z, dtype=jnp.int32)
    link = links.reshape((4, 4, slab_x, slab_z, LY, LT))
    field = gauge.reshape((4, slab_x, slab_z, LY, LT))
    parity = site_parity(coord_x, coord_z)
    from_below_x = from_behind(link[:, 0, slab_x - 1 :], "wide", 1)
    from_below_z = from_behind(link[:, 2, :, slab_z - 1 :], "narrow", 1)
    behind_links = [
        jnp.concatenate([from_below_x, link[:, 0, : slab_x - 1]], axis=1),
        jnp.roll(link[:, 1], 1, axis=3),
        jnp.concatenate([from_below_z, link[:, 2, :, : slab_z - 1]], axis=2),
        jnp.roll(link[:, 3], 1, axis=4),
    ]
    for half_sweep in range(HALF_SWEEPS):
        update_side = half_sweep % 2
        padded = padded_2(field, (("wide", 1), ("narrow", 2)), 1)
        center = padded[:, 1:-1, 1:-1]
        ahead_list = [
            padded[:, 2:, 1:-1],
            jnp.roll(center, -1, axis=3),
            padded[:, 1:-1, 2:],
            jnp.roll(center, -1, axis=4),
        ]
        behind_list = [
            padded[:, :-2, 1:-1],
            jnp.roll(center, 1, axis=3),
            padded[:, 1:-1, :-2],
            jnp.roll(center, 1, axis=4),
        ]
        kernel_sum = jnp.zeros(field.shape, jnp.float32)
        for direction in range(4):
            kernel_sum = (
                kernel_sum
                + quat_product(link[:, direction], quat_conj(ahead_list[direction]))
                + quat_product(
                    quat_conj(behind_links[direction]), quat_conj(behind_list[direction])
                )
            )
        field = jnp.where((parity == update_side)[None], relax_sites(field, kernel_sum), field)
    next_x = from_behind(field[:, :1], "wide", -1)
    next_z = from_behind(field, "narrow", -1)
    forward_list = [
        jnp.concatenate([field[:, 1:], next_x], axis=1),
        jnp.roll(field, -1, axis=3),
        jnp.concatenate([field[:, :, 1:], next_z], axis=2),
        jnp.roll(field, -1, axis=4),
    ]
    pieces = []
    for direction in range(4):
        transformed = quat_product(
            quat_product(field, link[:, direction]), quat_conj(forward_list[direction])
        )
        pieces.append(transformed[1:])
    potential = jnp.stack(pieces, axis=1).reshape((12, slab_x, slab_z, LY, LT))
    cosine_t, sine_t = fourier_tables(LT)
    real_part = jnp.matmul(potential, cosine_t, precision=lax.Precision.HIGHEST)
    imag_part = -jnp.matmul(potential, sine_t, precision=lax.Precision.HIGHEST)
    spectrum = along_axis(jnp.stack([real_part, imag_part]), 4)
    spectrum = along_x(lax.all_to_all(spectrum, "wide", split_axis=4, concat_axis=2, tiled=True))
    spectrum = along_z(lax.all_to_all(spectrum, "narrow", split_axis=5, concat_axis=3, tiled=True))
    scale = float(count_wide * slab_x * count_narrow * slab_z * LY * LT) ** (-0.5)
    spectrum = spectrum * scale
    full_x = spectrum.shape[2]
    full_z = spectrum.shape[3]
    spectrum = jnp.transpose(spectrum, (0, 1, 4, 5, 2, 3))
    spectrum = spectrum.reshape((2, 12, spectrum.shape[2], spectrum.shape[3], full_x * full_z))
    return (spectrum, field.reshape((4, slab_x, slab_z, LY * LT)))


ROWS = 8
INNER = LY // ROWS
LANES = INNER * LT
COMPS = 12
MESH = pl.DeviceIdType.MESH


def split_pair(table):
    high = table.astype(jnp.bfloat16)
    low = (table - high.astype(np.float32)).astype(jnp.bfloat16)
    return np.stack([np.asarray(high), np.asarray(low)])


def make_tables(wide, narrow, slab_x):
    turn = 2.0 * np.pi
    per_kt = LT // narrow
    k0 = np.arange(ROWS)
    angle = turn * (np.outer(k0, k0) % ROWS) / ROWS
    first = np.zeros((2, 16, ROWS, COMPS, ROWS))
    for c in range(COMPS):
        first[0, c, :, c, :] = np.cos(angle)
        first[1, c, :, c, :] = -np.sin(angle)
    first = first.reshape(256, COMPS * ROWS)
    inner = np.repeat(np.arange(INNER), LT)
    angle = turn * np.outer(k0, inner) / LY
    twiddle = np.stack([np.cos(angle), np.sin(angle)])
    time = np.tile(np.arange(LT), INNER)
    kb = np.arange(wide)
    kt = np.arange(LT)
    part_b = np.exp(-1j * turn * (np.outer(kb, inner) % wide) / wide)
    part_t = np.exp(-1j * turn * (np.outer(kt, time) % LT) / LT)
    phase = (part_b[:, None, :] * part_t[None]).reshape(wide, narrow, per_kt, LANES)
    second = np.empty((wide, narrow, 2, per_kt, 2, LANES))
    second[:, :, 0, :, 0] = phase.real
    second[:, :, 0, :, 1] = -phase.imag
    second[:, :, 1, :, 0] = phase.imag
    second[:, :, 1, :, 1] = phase.real
    second = second.reshape(wide * narrow * 2 * per_kt, 2 * LANES)
    nx = wide * slab_x
    kx = np.arange(nx)
    kz = np.arange(narrow)
    part_x = np.exp(-1j * turn * (np.outer(kx, kx) % nx) / nx).reshape(nx, wide, slab_x)
    part_z = np.exp(-1j * turn * (np.outer(kz, kz) % narrow) / narrow)
    phase = part_x[:, None, :, None, :] * part_z[None, :, None, :, None]
    phase = phase * float(nx * narrow * LY * LT) ** (-0.5)
    third = np.empty((2, nx, narrow, wide, narrow, slab_x, 2))
    third[0, ..., 0] = phase.real
    third[0, ..., 1] = -phase.imag
    third[1, ..., 0] = phase.imag
    third[1, ..., 1] = phase.real
    third = third.reshape(2 * nx * narrow, wide * narrow * slab_x * 2)
    f32 = np.float32
    return (
        split_pair(first.astype(f32)),
        twiddle.astype(f32),
        split_pair(second.astype(f32)),
        split_pair(third.astype(f32)),
    )


def qmul(a, b):
    return [
        a[0] * b[0] - a[1] * b[1] - a[2] * b[2] - a[3] * b[3],
        a[0] * b[1] + b[0] * a[1] - (a[2] * b[3] - a[3] * b[2]),
        a[0] * b[2] + b[0] * a[2] - (a[3] * b[1] - a[1] * b[3]),
        a[0] * b[3] + b[0] * a[3] - (a[1] * b[2] - a[2] * b[1]),
    ]


def qconj(a):
    return [a[0], -a[1], -a[2], -a[3]]


def qadd(a, b):
    return [p + q for p, q in zip(a, b)]


def qwhere(mask, a, b):
    return [jnp.where(mask, p, q) for p, q in zip(a, b)]


def qnorm(a):
    return jnp.sqrt(a[0] * a[0] + a[1] * a[1] + a[2] * a[2] + a[3] * a[3])


def halves(value):
    high = value.astype(jnp.bfloat16)
    return high, (value - high.astype(jnp.float32)).astype(jnp.bfloat16)


def dot3(pair_a, pair_b, dims):
    def one(a, b):
        return lax.dot_general(a, b, (dims, ((), ())), preferred_element_type=jnp.float32)

    return one(pair_a[0], pair_b[0]) + (one(pair_a[1], pair_b[0]) + one(pair_a[0], pair_b[1]))


def fused(
    wide, narrow,
    links_ref, gauge_ref, first_ref, twiddle_ref, second_hbm, third_ref,
    out_ref, field_ref,
    second_ref, face_out, face_in, pot, outgoing, arrived, turned,
    table_sem, face_send, face_recv, far_send, far_recv, own_sem,
):
    my_w = lax.axis_index("wide")
    my_n = lax.axis_index("narrow")
    per_kt = LT // narrow
    block = 4 * per_kt
    table_copy = pltpu.make_async_copy(second_hbm, second_ref, table_sem)
    table_copy.start()

    barrier = pltpu.get_barrier_semaphore()
    for i in range(wide):
        for k in range(narrow):
            if i or k:
                peer = (lax.rem(my_w + i, wide), lax.rem(my_n + k, narrow))
                pl.semaphore_signal(barrier, inc=1, device_id=peer, device_id_type=MESH)

    lane = lax.broadcasted_iota(jnp.int32, (ROWS, LANES), 1)
    inner = jnp.zeros((ROWS, LANES), jnp.int32)
    for j in range(1, INNER):
        inner = inner + jnp.where(lane >= LT * j, 1, 0)
    time = lane - LT * inner
    even = ((my_n + inner + time) & 1) == 0
    odd = jnp.logical_not(even)
    first_t, last_t = time == 0, time == LT - 1
    first_j, last_j = inner == 0, inner == INNER - 1

    def ahead_t(v):
        return jnp.where(last_t, pltpu.roll(v, LT - 1, 1), pltpu.roll(v, LANES - 1, 1))

    def behind_t(v):
        return jnp.where(first_t, pltpu.roll(v, LANES - LT + 1, 1), pltpu.roll(v, 1, 1))

    def ahead_y(v):
        moved = pltpu.roll(v, LANES - LT, 1)
        return jnp.where(last_j, pltpu.roll(moved, ROWS - 1, 0), moved)

    def behind_y(v):
        moved = pltpu.roll(v, LT, 1)
        return jnp.where(first_j, pltpu.roll(moved, 1, 0), moved)

    def tile(ref, index):
        return jnp.concatenate(
            [ref[pl.ds(index * 24 + s, ROWS, stride=3), :] for s in range(3)], axis=1
        )

    def both(ref, index_zero):
        zero, one = tile(ref, index_zero), tile(ref, index_zero + 1)
        return jnp.where(even, zero, one), jnp.where(even, one, zero)

    link = [[None] * 4, [None] * 4]
    for mu in range(4):
        pairs = [both(links_ref, (a * 4 + mu) * 2) for a in range(4)]
        for p in range(2):
            link[p][mu] = [pair[p] for pair in pairs]
    pairs = [both(gauge_ref, a * 2) for a in range(4)]
    field = [[pair[p] for pair in pairs] for p in range(2)]

    def neighbour(step_w, step_n):
        return (
            lax.rem(my_w + step_w + wide, wide),
            lax.rem(my_n + step_n + narrow, narrow),
        )

    def send_face(source, slot, step_w, step_n):
        copy = pltpu.make_async_remote_copy(
            src_ref=face_out.at[source],
            dst_ref=face_in.at[slot],
            send_sem=face_send.at[slot],
            recv_sem=face_recv.at[slot],
            device_id=neighbour(step_w, step_n),
            device_id_type=MESH,
        )
        copy.start()
        return copy

    def put_face(source, value):
        for a in range(4):
            face_out[source, a] = value[a]

    def got_face(slot):
        return [face_in[slot, a] for a in range(4)]

    copies = []
    moved_links = None
    kept_x = kept_z = None
    for half in range(HALF_SWEEPS):
        p = half % 2
        here = even if p == 0 else odd
        other = field[1 - p]
        moved_links = [qmul(other, link[1 - p][mu]) for mu in range(4)]
        put_face(3 * half, other)
        put_face(3 * half + 1, moved_links[0])
        put_face(3 * half + 2, moved_links[2])
        if half == 0:
            pl.semaphore_wait(barrier, wide * narrow - 1)
        started = [
            send_face(3 * half, 4 * half, -1, 0),
            send_face(3 * half, 4 * half + 1, 0, -1),
            send_face(3 * half + 1, 4 * half + 2, 1, 0),
            send_face(3 * half + 2, 4 * half + 3, 0, 1),
        ]
        copies += started
        total = qmul([ahead_y(v) for v in other], qconj(link[p][1]))
        total = qadd(total, [behind_y(v) for v in moved_links[1]])
        total = qadd(total, qmul([ahead_t(v) for v in other], qconj(link[p][3])))
        total = qadd(total, [behind_t(v) for v in moved_links[3]])
        for copy in started:
            copy.wait_recv()
        kept_x, kept_z = got_face(4 * half), got_face(4 * half + 1)
        total = qadd(total, qmul(qwhere(here, other, kept_x), qconj(link[p][0])))
        total = qadd(total, qmul(kept_z, qconj(link[p][2])))
        total = qadd(total, qwhere(here, got_face(4 * half + 2), moved_links[0]))
        total = qadd(total, got_face(4 * half + 3))
        centre = field[p]
        relaxed = [OMEGA * v for v in qmul(total, qconj(centre))]
        relaxed[0] = relaxed[0] + (1.0 - OMEGA) * qnorm(total)
        bound = jnp.maximum(qnorm(relaxed), 1.0)
        field[p] = [v / bound for v in qmul(relaxed, centre)]

    p = (HALF_SWEEPS - 1) % 2
    source, slot = 3 * HALF_SWEEPS, 4 * HALF_SWEEPS
    put_face(source, field[p])
    started = [send_face(source, slot, -1, 0), send_face(source, slot + 1, 0, -1)]
    copies += started
    for a in range(4):
        zero = jnp.where(even, field[0][a], field[1][a])
        one = jnp.where(even, field[1][a], field[0][a])
        for x, value in enumerate((zero, one)):
            for s in range(3):
                field_ref[pl.ds((a * 2 + x) * 24 + s, ROWS, stride=3), :] = value[
                    :, 128 * s : 128 * (s + 1)
                ]
    carried = [None, None]
    carried[1 - p] = moved_links
    carried[p] = [qmul(field[p], link[p][mu]) for mu in range(4)]
    here = even if p == 0 else odd

    def put_potential(mu, ahead):
        value = [qmul(carried[q][mu], qconj(ahead[q])) for q in range(2)]
        for a in range(3):
            c = 4 * a + mu
            zero = jnp.where(even, value[0][a + 1], value[1][a + 1])
            one = jnp.where(even, value[1][a + 1], value[0][a + 1])
            pot[0, c * ROWS : (c + 1) * ROWS, :] = zero
            pot[1, c * ROWS : (c + 1) * ROWS, :] = one

    put_potential(1, [[ahead_y(v) for v in field[1 - q]] for q in range(2)])
    put_potential(3, [[ahead_t(v) for v in field[1 - q]] for q in range(2)])
    for copy in started:
        copy.wait_recv()
    fresh_x, fresh_z = got_face(slot), got_face(slot + 1)
    there = odd if p == 0 else even
    ahead = [None, None]
    ahead[p] = qwhere(here, field[1 - p], kept_x)
    ahead[1 - p] = qwhere(there, field[p], fresh_x)
    put_potential(0, ahead)
    ahead[p], ahead[1 - p] = kept_z, fresh_z
    put_potential(2, ahead)

    first = (first_ref[0], first_ref[1])
    cosine, sine = twiddle_ref[0][None], twiddle_ref[1][None]
    highs, lows = [], []
    for x in range(2):
        turned_r = dot3(first, halves(pot[x]), ((1,), (0,))).reshape(2, 16, ROWS, LANES)
        real = turned_r[0] * cosine + turned_r[1] * sine
        imag = turned_r[1] * cosine - turned_r[0] * sine
        both_parts = jnp.concatenate(
            [real.reshape(128, LANES), imag.reshape(128, LANES)], axis=1
        )
        high, low = halves(both_parts)
        highs.append(high)
        lows.append(low)
    mid = (jnp.concatenate(highs, axis=0), jnp.concatenate(lows, axis=0))
    table_copy.wait()
    per_b = narrow * 2 * per_kt
    group = 2
    for g in range(wide // group):
        rows = slice(g * group * per_b, (g + 1) * group * per_b)
        value = dot3((second_ref[0, rows, :], second_ref[1, rows, :]), mid, ((1,), (1,)))
        for m in range(group * narrow):
            target = g * group * narrow + m
            for x in range(2):
                outgoing[target * block + x * 2 * per_kt : target * block + (x + 1) * 2 * per_kt, :] = (
                    value[m * 2 * per_kt : (m + 1) * 2 * per_kt, 128 * x : 128 * (x + 1)]
                )

    def span(w, n):
        return pl.ds(pl.multiple_of((w * narrow + n) * block, 8), block)

    mine = span(my_w, my_n)
    for i in range(wide):
        for k in range(narrow):
            if i or k:
                w, n = lax.rem(my_w + i, wide), lax.rem(my_n + k, narrow)
                copy = pltpu.make_async_remote_copy(
                    src_ref=outgoing.at[span(w, n)],
                    dst_ref=arrived.at[mine],
                    send_sem=far_send.at[i * narrow + k],
                    recv_sem=far_recv.at[i * narrow + k],
                    device_id=(w, n),
                    device_id_type=MESH,
                )
                copy.start()
                copies.append(copy)
    own = pltpu.make_async_copy(outgoing.at[mine], arrived.at[mine], own_sem)
    own.start()
    own.wait()
    for i in range(wide):
        for k in range(narrow):
            if i or k:
                w, n = lax.rem(my_w + wide - i, wide), lax.rem(my_n + narrow - k, narrow)
                pltpu.make_async_remote_copy(
                    src_ref=outgoing.at[span(w, n)],
                    dst_ref=arrived.at[span(w, n)],
                    send_sem=far_send.at[i * narrow + k],
                    recv_sem=far_recv.at[i * narrow + k],
                    device_id=(w, n),
                    device_id_type=MESH,
                ).wait_recv()

    third = (third_ref[0], third_ref[1])
    momenta = third_ref.shape[1] // 2
    depth = third_ref.shape[2]
    for kt in range(per_kt):
        value = halves(arrived[pl.ds(kt, depth, stride=per_kt), :])
        turned[kt * 128 : (kt + 1) * 128, :] = dot3(third, value, ((1,), (0,))).T
    for c in range(COMPS):
        for k0 in range(ROWS):
            value = turned[pl.ds(c * ROWS + k0, per_kt, stride=128), :]
            out_ref[0, c, k0] = value[:, :momenta]
            out_ref[1, c, k0] = value[:, momenta:]
    for copy in copies:
        copy.wait_send()


def fused_body(wide, narrow, links, gauge):
    slab_x = gauge.shape[1]
    tables = make_tables(wide, narrow, slab_x)
    devices = wide * narrow
    per_kt = LT // narrow
    block = 4 * per_kt
    faces = 4 * HALF_SWEEPS + 2
    vmem = pl.BlockSpec(memory_space=pltpu.VMEM)
    spectrum, field = pl.pallas_call(
        lambda *refs: fused(wide, narrow, *refs),
        out_shape=(
            jax.ShapeDtypeStruct((2, COMPS, ROWS, per_kt, wide * slab_x * narrow), jnp.float32),
            jax.ShapeDtypeStruct((4 * slab_x * 24, 128), jnp.float32),
        ),
        in_specs=[vmem, vmem, vmem, vmem, pl.BlockSpec(memory_space=pl.ANY), vmem],
        out_specs=(vmem, vmem),
        scratch_shapes=[
            pltpu.VMEM(tables[2].shape, jnp.bfloat16),
            pltpu.VMEM((3 * HALF_SWEEPS + 1, 4, ROWS, LANES), jnp.float32),
            pltpu.VMEM((faces, 4, ROWS, LANES), jnp.float32),
            pltpu.VMEM((2, COMPS * ROWS, LANES), jnp.float32),
            pltpu.VMEM((devices * block, 128), jnp.float32),
            pltpu.VMEM((devices * block, 128), jnp.float32),
            pltpu.VMEM((per_kt * 128, 128), jnp.float32),
            pltpu.SemaphoreType.DMA,
            pltpu.SemaphoreType.DMA((faces,)),
            pltpu.SemaphoreType.DMA((faces,)),
            pltpu.SemaphoreType.DMA((devices,)),
            pltpu.SemaphoreType.DMA((devices,)),
            pltpu.SemaphoreType.DMA,
        ],
        compiler_params=pltpu.CompilerParams(
            collective_id=0, has_side_effects=True, vmem_limit_bytes=40 * 1024 * 1024
        ),
    )(
        links.reshape(4 * 4 * slab_x * 24, 128),
        gauge.reshape(4 * slab_x * 24, 128),
        *[jnp.asarray(table) for table in tables],
    )
    return spectrum, field.reshape(gauge.shape)


def solution(mesh):
    in_specs = (P(None, None, "wide", "narrow", None), P(None, "wide", "narrow", None))
    out_specs = (P(None, None, "wide", "narrow", None), P(None, "wide", "narrow", None))
    wide, narrow = mesh.shape["wide"], mesh.shape["narrow"]

    def per_device(links, gauge):
        slab_x, slab_z = gauge.shape[1:3]
        fits = slab_x == 2 and slab_z == 1 and wide * ROWS == LY and wide * narrow * 4 == 128
        if fits:
            return fused_body(wide, narrow, links, gauge)
        return body(links, gauge)

    return jax.shard_map(
        per_device, mesh=mesh, in_specs=in_specs, out_specs=out_specs, check_vma=False
    )
```

```python
import math

import jax
import jax.numpy as jnp
import numpy as np
from jax import lax
from jax.experimental import pallas as pl
from jax.experimental.pallas import tpu as pltpu
from jax.sharding import PartitionSpec as P

LY = 64
LT = 48
HALF_SWEEPS = 2


OMEGA = 1.7


def from_behind(value, axis, steps):
    count = lax.axis_size(axis)
    pairs = [(source, (source + steps) % count) for source in range(count)]
    return lax.ppermute(value, axis, pairs)


def padded_2(block, sides, width):
    for axis, dim in sides:
        count = lax.axis_size(axis)
        forward = [(i, i + 1) for i in range(count - 1)]
        forward.append((count - 1, 0))
        backward = [(target, source) for source, target in forward]
        low = lax.ppermute(
            lax.slice_in_dim(block, block.shape[dim] - width, None, axis=dim), axis, forward
        )
        high = lax.ppermute(lax.slice_in_dim(block, 0, width, axis=dim), axis, backward)
        block = jnp.concatenate([low, block, high], axis=dim)
    return block


def quat_product(first_quat, second_quat):
    scalar = (
        first_quat[0] * second_quat[0]
        - first_quat[1] * second_quat[1]
        - first_quat[2] * second_quat[2]
        - first_quat[3] * second_quat[3]
    )
    vector_one = (
        first_quat[0] * second_quat[1]
        + second_quat[0] * first_quat[1]
        - (first_quat[2] * second_quat[3] - first_quat[3] * second_quat[2])
    )
    vector_two = (
        first_quat[0] * second_quat[2]
        + second_quat[0] * first_quat[2]
        - (first_quat[3] * second_quat[1] - first_quat[1] * second_quat[3])
    )
    vector_three = (
        first_quat[0] * second_quat[3]
        + second_quat[0] * first_quat[3]
        - (first_quat[1] * second_quat[2] - first_quat[2] * second_quat[1])
    )
    return jnp.stack([scalar, vector_one, vector_two, vector_three])


def quat_conj(quaternion):
    return jnp.concatenate([quaternion[:1], -quaternion[1:]], axis=0)


def relax_sites(field, kernel_sum):
    kernel_norm = jnp.sqrt(jnp.sum(kernel_sum * kernel_sum, axis=0))
    rotated = OMEGA * quat_product(quat_conj(kernel_sum), quat_conj(field))
    relaxed = jnp.concatenate(
        [rotated[:1] + (1.0 - OMEGA) * kernel_norm[None], rotated[1:]], axis=0
    )
    relaxed_norm = jnp.sqrt(jnp.sum(relaxed * relaxed, axis=0))
    return quat_product(relaxed, field) / jnp.maximum(relaxed_norm, 1.0)[None]


def site_parity(coord_x, coord_z):
    rows_y = jnp.arange(LY, dtype=jnp.int32)
    rows_t = jnp.arange(LT, dtype=jnp.int32)
    return (
        coord_x[:, None, None, None]
        + coord_z[None, :, None, None]
        + rows_y[None, None, :, None]
        + rows_t[None, None, None, :]
    ) % 2


def fourier_tables(length):
    indices = jnp.arange(length, dtype=jnp.int32)
    phases = indices[:, None] * indices[None, :] % length
    angles = phases.astype(jnp.float32) * (2.0 * math.pi / length)
    return (jnp.cos(angles), jnp.sin(angles))


def along_axis(spectrum, axis_number):
    cosine, sine_part = fourier_tables(spectrum.shape[axis_number])
    moved_last = jnp.moveaxis(spectrum, axis_number, -1)
    cos_term = jnp.matmul(moved_last, cosine, precision=lax.Precision.HIGHEST)
    sin_term = jnp.matmul(moved_last, sine_part, precision=lax.Precision.HIGHEST)
    rotated = jnp.stack([cos_term[0] + sin_term[1], cos_term[1] - sin_term[0]])
    return jnp.moveaxis(rotated, -1, axis_number)


def along_x(spectrum):
    return along_axis(spectrum, 2)


def along_z(spectrum):
    return along_axis(spectrum, 3)


def body(links, gauge):
    slab_x = gauge.shape[1]
    slab_z = gauge.shape[2]
    count_wide = lax.axis_size("wide")
    count_narrow = lax.axis_size("narrow")
    coord_x = lax.axis_index("wide") * slab_x + jnp.arange(slab_x, dtype=jnp.int32)
    coord_z = lax.axis_index("narrow") * slab_z + jnp.arange(slab_z, dtype=jnp.int32)
    link = links.reshape((4, 4, slab_x, slab_z, LY, LT))
    field = gauge.reshape((4, slab_x, slab_z, LY, LT))
    parity = site_parity(coord_x, coord_z)
    from_below_x = from_behind(link[:, 0, slab_x - 1 :], "wide", 1)
    from_below_z = from_behind(link[:, 2, :, slab_z - 1 :], "narrow", 1)
    behind_links = [
        jnp.concatenate([from_below_x, link[:, 0, : slab_x - 1]], axis=1),
        jnp.roll(link[:, 1], 1, axis=3),
        jnp.concatenate([from_below_z, link[:, 2, :, : slab_z - 1]], axis=2),
        jnp.roll(link[:, 3], 1, axis=4),
    ]
    for half_sweep in range(HALF_SWEEPS):
        update_side = half_sweep % 2
        padded = padded_2(field, (("wide", 1), ("narrow", 2)), 1)
        center = padded[:, 1:-1, 1:-1]
        ahead_list = [
            padded[:, 2:, 1:-1],
            jnp.roll(center, -1, axis=3),
            padded[:, 1:-1, 2:],
            jnp.roll(center, -1, axis=4),
        ]
        behind_list = [
            padded[:, :-2, 1:-1],
            jnp.roll(center, 1, axis=3),
            padded[:, 1:-1, :-2],
            jnp.roll(center, 1, axis=4),
        ]
        kernel_sum = jnp.zeros(field.shape, jnp.float32)
        for direction in range(4):
            kernel_sum = (
                kernel_sum
                + quat_product(link[:, direction], quat_conj(ahead_list[direction]))
                + quat_product(
                    quat_conj(behind_links[direction]), quat_conj(behind_list[direction])
                )
            )
        field = jnp.where((parity == update_side)[None], relax_sites(field, kernel_sum), field)
    next_x = from_behind(field[:, :1], "wide", -1)
    next_z = from_behind(field, "narrow", -1)
    forward_list = [
        jnp.concatenate([field[:, 1:], next_x], axis=1),
        jnp.roll(field, -1, axis=3),
        jnp.concatenate([field[:, :, 1:], next_z], axis=2),
        jnp.roll(field, -1, axis=4),
    ]
    pieces = []
    for direction in range(4):
        transformed = quat_product(
            quat_product(field, link[:, direction]), quat_conj(forward_list[direction])
        )
        pieces.append(transformed[1:])
    potential = jnp.stack(pieces, axis=1).reshape((12, slab_x, slab_z, LY, LT))
    cosine_t, sine_t = fourier_tables(LT)
    real_part = jnp.matmul(potential, cosine_t, precision=lax.Precision.HIGHEST)
    imag_part = -jnp.matmul(potential, sine_t, precision=lax.Precision.HIGHEST)
    spectrum = along_axis(jnp.stack([real_part, imag_part]), 4)
    spectrum = along_x(lax.all_to_all(spectrum, "wide", split_axis=4, concat_axis=2, tiled=True))
    spectrum = along_z(lax.all_to_all(spectrum, "narrow", split_axis=5, concat_axis=3, tiled=True))
    scale = float(count_wide * slab_x * count_narrow * slab_z * LY * LT) ** (-0.5)
    spectrum = spectrum * scale
    full_x = spectrum.shape[2]
    full_z = spectrum.shape[3]
    spectrum = jnp.transpose(spectrum, (0, 1, 4, 5, 2, 3))
    spectrum = spectrum.reshape((2, 12, spectrum.shape[2], spectrum.shape[3], full_x * full_z))
    return (spectrum, field.reshape((4, slab_x, slab_z, LY * LT)))


ROWS = 8
INNER = LY // ROWS
LANES = INNER * LT
COMPS = 12
VMEM_MIB = 60
MESH = pl.DeviceIdType.MESH


def split_pair(table):
    high = table.astype(jnp.bfloat16)
    low = (table - high.astype(np.float32)).astype(jnp.bfloat16)
    return np.stack([np.asarray(high), np.asarray(low)])


def make_tables(wide, narrow, slab_x):
    turn = 2.0 * np.pi
    per_kt = LT // narrow
    k0 = np.arange(ROWS)
    angle = turn * (np.outer(k0, k0) % ROWS) / ROWS
    first = np.zeros((2, 16, ROWS, COMPS, ROWS))
    for c in range(COMPS):
        first[0, c, :, c, :] = np.cos(angle)
        first[1, c, :, c, :] = -np.sin(angle)
    first = first.reshape(256, COMPS * ROWS)
    inner = np.repeat(np.arange(INNER), LT)
    angle = turn * np.outer(k0, inner) / LY
    twiddle = np.stack([np.cos(angle), np.sin(angle)])
    time = np.tile(np.arange(LT), INNER)
    kb = np.arange(wide)
    kt = np.arange(LT)
    part_b = np.exp(-1j * turn * (np.outer(kb, inner) % wide) / wide)
    part_t = np.exp(-1j * turn * (np.outer(kt, time) % LT) / LT)
    phase = (part_b[:, None, :] * part_t[None]).reshape(wide, narrow, per_kt, LANES)
    second = np.empty((wide, narrow, 2, per_kt, 2, LANES))
    second[:, :, 0, :, 0] = phase.real
    second[:, :, 0, :, 1] = -phase.imag
    second[:, :, 1, :, 0] = phase.imag
    second[:, :, 1, :, 1] = phase.real
    second = second.transpose(0, 2, 1, 3, 4, 5).reshape(wide * narrow * 2 * per_kt, 2 * LANES)
    nx = wide * slab_x
    kx = np.arange(nx)
    kz = np.arange(narrow)
    part_x = np.exp(-1j * turn * (np.outer(kx, kx) % nx) / nx).reshape(nx, wide, slab_x)
    part_z = np.exp(-1j * turn * (np.outer(kz, kz) % narrow) / narrow)
    phase = part_x[:, None, :, None, :] * part_z[None, :, None, :, None]
    phase = phase * float(nx * narrow * LY * LT) ** (-0.5)
    third = np.empty((2, nx, narrow, wide, narrow, slab_x, 2))
    third[0, ..., 0] = phase.real
    third[0, ..., 1] = -phase.imag
    third[1, ..., 0] = phase.imag
    third[1, ..., 1] = phase.real
    third = third.transpose(0, 1, 2, 5, 6, 3, 4).reshape(2 * nx * narrow, wide * narrow * slab_x * 2)
    f32 = np.float32
    return (
        split_pair(first.astype(f32)),
        twiddle.astype(f32),
        split_pair(second.astype(f32)),
        split_pair(third.astype(f32)),
    )


def qmul(a, b):
    return [
        a[0] * b[0] - a[1] * b[1] - a[2] * b[2] - a[3] * b[3],
        a[0] * b[1] + b[0] * a[1] - (a[2] * b[3] - a[3] * b[2]),
        a[0] * b[2] + b[0] * a[2] - (a[3] * b[1] - a[1] * b[3]),
        a[0] * b[3] + b[0] * a[3] - (a[1] * b[2] - a[2] * b[1]),
    ]


def qconj(a):
    return [a[0], -a[1], -a[2], -a[3]]


def qadd(a, b):
    return [p + q for p, q in zip(a, b)]


def qwhere(mask, a, b):
    return [jnp.where(mask, p, q) for p, q in zip(a, b)]


def qnorm(a):
    return jnp.sqrt(a[0] * a[0] + a[1] * a[1] + a[2] * a[2] + a[3] * a[3])


def halves(value):
    high = value.astype(jnp.bfloat16)
    return high, (value - high.astype(jnp.float32)).astype(jnp.bfloat16)


def dot3(pair_a, pair_b, dims):
    def one(a, b):
        return lax.dot_general(a, b, (dims, ((), ())), preferred_element_type=jnp.float32)

    return one(pair_a[0], pair_b[0]) + (one(pair_a[1], pair_b[0]) + one(pair_a[0], pair_b[1]))


def fused(
    wide, narrow,
    links_hbm, gauge_hbm, first_hbm, twiddle_hbm, second_hbm, third_hbm,
    out_ref, field_ref,
    links_ref, gauge_ref, first_ref, twiddle_ref, second_ref, third_ref,
    face_out, face_in, pot, outgoing, arrived,
    load_sem, face_send, face_recv, far_send, far_recv, own_sem,
):
    my_w = lax.axis_index("wide")
    my_n = lax.axis_index("narrow")
    per_kt = LT // narrow
    loads = [
        pltpu.make_async_copy(source, target, load_sem.at[i])
        for i, (source, target) in enumerate(
            [
                (links_hbm, links_ref),
                (gauge_hbm, gauge_ref),
                (first_hbm, first_ref),
                (twiddle_hbm, twiddle_ref),
                (third_hbm, third_ref),
                (second_hbm, second_ref),
            ]
        )
    ]
    for load in loads:
        load.start()

    barrier = pltpu.get_barrier_semaphore()
    for i in range(wide):
        for k in range(narrow):
            if i or k:
                peer = (lax.rem(my_w + i, wide), lax.rem(my_n + k, narrow))
                pl.semaphore_signal(barrier, inc=1, device_id=peer, device_id_type=MESH)

    lane = lax.broadcasted_iota(jnp.int32, (ROWS, LANES), 1)
    inner = jnp.zeros((ROWS, LANES), jnp.int32)
    for j in range(1, INNER):
        inner = inner + jnp.where(lane >= LT * j, 1, 0)
    time = lane - LT * inner
    even = ((my_n + inner + time) & 1) == 0
    odd = jnp.logical_not(even)
    first_t, last_t = time == 0, time == LT - 1
    first_j, last_j = inner == 0, inner == INNER - 1

    def ahead_t(v):
        return jnp.where(last_t, pltpu.roll(v, LT - 1, 1), pltpu.roll(v, LANES - 1, 1))

    def behind_t(v):
        return jnp.where(first_t, pltpu.roll(v, LANES - LT + 1, 1), pltpu.roll(v, 1, 1))

    def ahead_y(v):
        moved = pltpu.roll(v, LANES - LT, 1)
        return jnp.where(last_j, pltpu.roll(moved, ROWS - 1, 0), moved)

    def behind_y(v):
        moved = pltpu.roll(v, LT, 1)
        return jnp.where(first_j, pltpu.roll(moved, 1, 0), moved)

    def tile(ref, index):
        return jnp.concatenate(
            [ref[pl.ds(index * 24 + s, ROWS, stride=3), :] for s in range(3)], axis=1
        )

    def both(ref, index_zero):
        zero, one = tile(ref, index_zero), tile(ref, index_zero + 1)
        return jnp.where(even, zero, one), jnp.where(even, one, zero)

    loads[0].wait()
    loads[1].wait()
    link = [[None] * 4, [None] * 4]
    for mu in range(4):
        pairs = [both(links_ref, (a * 4 + mu) * 2) for a in range(4)]
        for p in range(2):
            link[p][mu] = [pair[p] for pair in pairs]
    pairs = [both(gauge_ref, a * 2) for a in range(4)]
    field = [[pair[p] for pair in pairs] for p in range(2)]

    def neighbour(step_w, step_n):
        return (
            lax.rem(my_w + step_w + wide, wide),
            lax.rem(my_n + step_n + narrow, narrow),
        )

    def send_face(source, slot, step_w, step_n):
        copy = pltpu.make_async_remote_copy(
            src_ref=face_out.at[source],
            dst_ref=face_in.at[slot],
            send_sem=face_send.at[slot],
            recv_sem=face_recv.at[slot],
            device_id=neighbour(step_w, step_n),
            device_id_type=MESH,
        )
        copy.start()
        return copy

    def put_face(source, value):
        for a in range(4):
            face_out[source, a] = value[a]

    def got_face(slot):
        return [face_in[slot, a] for a in range(4)]

    copies = []
    moved_links = None
    kept_x = kept_z = None
    for half in range(HALF_SWEEPS):
        p = half % 2
        here = even if p == 0 else odd
        other = field[1 - p]
        moved_links = [qmul(other, link[1 - p][mu]) for mu in range(4)]
        put_face(3 * half, other)
        put_face(3 * half + 1, moved_links[0])
        put_face(3 * half + 2, moved_links[2])
        if half == 0:
            pl.semaphore_wait(barrier, wide * narrow - 1)
        started = [
            send_face(3 * half, 4 * half, -1, 0),
            send_face(3 * half, 4 * half + 1, 0, -1),
            send_face(3 * half + 1, 4 * half + 2, 1, 0),
            send_face(3 * half + 2, 4 * half + 3, 0, 1),
        ]
        copies += started
        total = qmul([ahead_y(v) for v in other], qconj(link[p][1]))
        total = qadd(total, [behind_y(v) for v in moved_links[1]])
        total = qadd(total, qmul([ahead_t(v) for v in other], qconj(link[p][3])))
        total = qadd(total, [behind_t(v) for v in moved_links[3]])
        for copy in started:
            copy.wait_recv()
        kept_x, kept_z = got_face(4 * half), got_face(4 * half + 1)
        total = qadd(total, qmul(qwhere(here, other, kept_x), qconj(link[p][0])))
        total = qadd(total, qmul(kept_z, qconj(link[p][2])))
        total = qadd(total, qwhere(here, got_face(4 * half + 2), moved_links[0]))
        total = qadd(total, got_face(4 * half + 3))
        centre = field[p]
        relaxed = [OMEGA * v for v in qmul(total, qconj(centre))]
        relaxed[0] = relaxed[0] + (1.0 - OMEGA) * qnorm(total)
        bound = jnp.maximum(qnorm(relaxed), 1.0)
        field[p] = [v / bound for v in qmul(relaxed, centre)]

    p = (HALF_SWEEPS - 1) % 2
    source, slot = 3 * HALF_SWEEPS, 4 * HALF_SWEEPS
    put_face(source, field[p])
    started = [send_face(source, slot, -1, 0), send_face(source, slot + 1, 0, -1)]
    copies += started
    for a in range(4):
        zero = jnp.where(even, field[0][a], field[1][a])
        one = jnp.where(even, field[1][a], field[0][a])
        for x, value in enumerate((zero, one)):
            for s in range(3):
                field_ref[pl.ds((a * 2 + x) * 24 + s, ROWS, stride=3), :] = value[
                    :, 128 * s : 128 * (s + 1)
                ]
    carried = [None, None]
    carried[1 - p] = moved_links
    carried[p] = [qmul(field[p], link[p][mu]) for mu in range(4)]
    here = even if p == 0 else odd

    def put_potential(mu, ahead):
        value = [qmul(carried[q][mu], qconj(ahead[q])) for q in range(2)]
        for a in range(3):
            c = 4 * a + mu
            zero = jnp.where(even, value[0][a + 1], value[1][a + 1])
            one = jnp.where(even, value[1][a + 1], value[0][a + 1])
            pot[0, c * ROWS : (c + 1) * ROWS, :] = zero
            pot[1, c * ROWS : (c + 1) * ROWS, :] = one

    put_potential(1, [[ahead_y(v) for v in field[1 - q]] for q in range(2)])
    put_potential(3, [[ahead_t(v) for v in field[1 - q]] for q in range(2)])
    for copy in started:
        copy.wait_recv()
    fresh_x, fresh_z = got_face(slot), got_face(slot + 1)
    there = odd if p == 0 else even
    ahead = [None, None]
    ahead[p] = qwhere(here, field[1 - p], kept_x)
    ahead[1 - p] = qwhere(there, field[p], fresh_x)
    put_potential(0, ahead)
    ahead[p], ahead[1 - p] = kept_z, fresh_z
    put_potential(2, ahead)

    loads[2].wait()
    loads[3].wait()
    first = (first_ref[0], first_ref[1])
    cosine, sine = twiddle_ref[0][None], twiddle_ref[1][None]
    highs, lows = [], []
    for x in range(2):
        turned_r = dot3(first, halves(pot[x]), ((1,), (0,))).reshape(2, 16, ROWS, LANES)
        real = turned_r[0] * cosine + turned_r[1] * sine
        imag = turned_r[1] * cosine - turned_r[0] * sine
        both_parts = jnp.concatenate(
            [real.reshape(128, LANES), imag.reshape(128, LANES)], axis=1
        )
        high, low = halves(both_parts)
        highs.append(high)
        lows.append(low)
    used = COMPS * ROWS
    over = 128 - used

    def arrange(parts):
        zeros = jnp.zeros((over, 2 * LANES), jnp.bfloat16)
        return jnp.concatenate(
            [parts[0][:used], parts[1][:over], zeros, parts[1][over:used], zeros], axis=0
        )

    mid = (arrange(highs), arrange(lows))
    loads[5].wait()
    per_b = narrow * per_kt
    pair = 2
    groups = wide // pair
    block = message_rows(per_kt)
    my_z, my_x = my_w // pair, lax.rem(my_w, pair)

    def span(w, n):
        return pl.ds(pl.multiple_of((w * narrow + n) * block, 8), block)

    mine = span(my_w, my_n)
    steps = sorted(range(groups), key=lambda step: -min(step, groups - step))
    own = None
    for place, step in enumerate(steps):
        group = lax.rem(my_z + step, groups)
        rows = pl.ds(pl.multiple_of(group * (pair * 2 * per_b), 16), pair * 2 * per_b)
        value = dot3((second_ref[0, rows, :], second_ref[1, rows, :]), mid, ((1,), (1,)))
        for q in range(pair):
            real = value[q * 2 * per_b : q * 2 * per_b + per_b]
            imag = value[q * 2 * per_b + per_b : (q + 1) * 2 * per_b]
            extra = real[:, 128:] + pltpu.roll(imag[:, 128:], 64, 1)
            for n in range(narrow):
                base = ((place * pair + q) * narrow + n) * block
                take = slice(n * per_kt, (n + 1) * per_kt)
                outgoing[base : base + per_kt, :] = real[take, :128]
                outgoing[base + per_kt : base + 2 * per_kt, :] = imag[take, :128]
                outgoing[base + 2 * per_kt : base + 3 * per_kt, :] = extra[take]
                outgoing[base + 3 * per_kt : base + block, :] = jnp.zeros(
                    (block - 3 * per_kt, 128), jnp.float32
                )
        for q in range(pair):
            x = lax.rem(my_x + q, pair)
            for k in range(narrow):
                w, n = group * pair + x, lax.rem(my_n + k, narrow)
                index = (step * pair + q) * narrow + k
                held = pl.ds(
                    pl.multiple_of(((place * pair + x) * narrow + n) * block, 8), block
                )
                if index == 0:
                    own = pltpu.make_async_copy(outgoing.at[held], arrived.at[mine], own_sem)
                    own.start()
                    continue
                copy = pltpu.make_async_remote_copy(
                    src_ref=outgoing.at[held],
                    dst_ref=arrived.at[mine],
                    send_sem=far_send.at[index],
                    recv_sem=far_recv.at[index],
                    device_id=(w, n),
                    device_id_type=MESH,
                )
                copy.start()
                copies.append(copy)
    own.wait()
    loads[4].wait()
    for step in range(groups):
        for q in range(pair):
            for k in range(narrow):
                index = (step * pair + q) * narrow + k
                if index == 0:
                    continue
                w = lax.rem(my_z + groups - step, groups) * pair + lax.rem(my_x + q, pair)
                n = lax.rem(my_n + narrow - k, narrow)
                pltpu.make_async_remote_copy(
                    src_ref=outgoing.at[pl.ds(0, block)],
                    dst_ref=arrived.at[span(w, n)],
                    send_sem=far_send.at[index],
                    recv_sem=far_recv.at[index],
                    device_id=(w, n),
                    device_id_type=MESH,
                ).wait_recv()

    third = (third_ref[0], third_ref[1])
    devices = wide * narrow
    momenta = third_ref.shape[1] // 2
    start = lax.broadcasted_iota(jnp.int32, (devices, 128), 1) < over
    for kt in range(0, per_kt, 2):
        columns = []
        for m in range(2):
            real, imag, extra = [
                arrived[pl.ds(part * per_kt + kt + m, devices, stride=block), :]
                for part in range(3)
            ]
            real_one = jnp.where(start, pltpu.roll(real, over, 1), extra)
            imag_one = jnp.where(start, pltpu.roll(imag, over, 1), pltpu.roll(extra, 64, 1))
            columns.append(jnp.concatenate([real, imag, real_one, imag_one], axis=0))
        value = dot3(third, halves(jnp.concatenate(columns, axis=1)), ((1,), (0,)))
        for m in range(2):
            whole = value[:, 128 * m : 128 * (m + 1)].T[:used]
            out_ref[0, :, kt + m] = whole[:, :momenta].reshape(COMPS, ROWS, momenta)
            out_ref[1, :, kt + m] = whole[:, momenta:].reshape(COMPS, ROWS, momenta)
    for copy in copies:
        copy.wait_send()


def message_rows(per_kt):
    return -(-3 * per_kt // 8) * 8


def fused_body(wide, narrow, links, gauge):
    slab_x = gauge.shape[1]
    tables = make_tables(wide, narrow, slab_x)
    devices = wide * narrow
    per_kt = LT // narrow
    block = message_rows(per_kt)
    faces = 4 * HALF_SWEEPS + 2
    vmem = pl.BlockSpec(memory_space=pltpu.VMEM)
    operands = [
        links.reshape(4 * 4 * slab_x * 24, 128),
        gauge.reshape(4 * slab_x * 24, 128),
        *[jnp.asarray(table) for table in tables],
    ]
    spectrum, field = pl.pallas_call(
        lambda *refs: fused(wide, narrow, *refs),
        out_shape=(
            jax.ShapeDtypeStruct((2, COMPS, per_kt, ROWS, wide * slab_x * narrow), jnp.float32),
            jax.ShapeDtypeStruct((4 * slab_x * 24, 128), jnp.float32),
        ),
        in_specs=[pl.BlockSpec(memory_space=pl.ANY)] * len(operands),
        out_specs=(vmem, vmem),
        scratch_shapes=[
            *[pltpu.VMEM(value.shape, value.dtype) for value in operands],
            pltpu.VMEM((3 * HALF_SWEEPS + 1, 4, ROWS, LANES), jnp.float32),
            pltpu.VMEM((faces, 4, ROWS, LANES), jnp.float32),
            pltpu.VMEM((2, COMPS * ROWS, LANES), jnp.float32),
            pltpu.VMEM((devices * block, 128), jnp.float32),
            pltpu.VMEM((devices * block, 128), jnp.float32),
            pltpu.SemaphoreType.DMA((len(operands),)),
            pltpu.SemaphoreType.DMA((faces,)),
            pltpu.SemaphoreType.DMA((faces,)),
            pltpu.SemaphoreType.DMA((devices,)),
            pltpu.SemaphoreType.DMA((devices,)),
            pltpu.SemaphoreType.DMA,
        ],
        compiler_params=pltpu.CompilerParams(
            collective_id=0, has_side_effects=True, vmem_limit_bytes=VMEM_MIB * 1024 * 1024
        ),
    )(*operands)
    spectrum = jnp.transpose(spectrum, (0, 1, 3, 2, 4))
    return spectrum, field.reshape(gauge.shape)


def solution(mesh):
    in_specs = (P(None, None, "wide", "narrow", None), P(None, "wide", "narrow", None))
    out_specs = (P(None, None, "wide", "narrow", None), P(None, "wide", "narrow", None))
    wide, narrow = mesh.shape["wide"], mesh.shape["narrow"]

    def per_device(links, gauge):
        slab_x, slab_z = gauge.shape[1:3]
        fits = slab_x == 2 and slab_z == 1 and wide * ROWS == LY and wide * narrow * 4 == 128
        if fits:
            return fused_body(wide, narrow, links, gauge)
        return body(links, gauge)

    return jax.shard_map(
        per_device, mesh=mesh, in_specs=in_specs, out_specs=out_specs, check_vma=False
    )
```

```python
import math

import jax
import jax.numpy as jnp
import numpy as np
from jax import lax
from jax.experimental import pallas as pl
from jax.experimental.pallas import tpu as pltpu
from jax.sharding import PartitionSpec as P

LY = 64
LT = 48
HALF_SWEEPS = 2


OMEGA = 1.7


def from_behind(value, axis, steps):
    count = lax.axis_size(axis)
    pairs = [(source, (source + steps) % count) for source in range(count)]
    return lax.ppermute(value, axis, pairs)


def padded_2(block, sides, width):
    for axis, dim in sides:
        count = lax.axis_size(axis)
        forward = [(i, i + 1) for i in range(count - 1)]
        forward.append((count - 1, 0))
        backward = [(target, source) for source, target in forward]
        low = lax.ppermute(
            lax.slice_in_dim(block, block.shape[dim] - width, None, axis=dim), axis, forward
        )
        high = lax.ppermute(lax.slice_in_dim(block, 0, width, axis=dim), axis, backward)
        block = jnp.concatenate([low, block, high], axis=dim)
    return block


def quat_product(first_quat, second_quat):
    scalar = (
        first_quat[0] * second_quat[0]
        - first_quat[1] * second_quat[1]
        - first_quat[2] * second_quat[2]
        - first_quat[3] * second_quat[3]
    )
    vector_one = (
        first_quat[0] * second_quat[1]
        + second_quat[0] * first_quat[1]
        - (first_quat[2] * second_quat[3] - first_quat[3] * second_quat[2])
    )
    vector_two = (
        first_quat[0] * second_quat[2]
        + second_quat[0] * first_quat[2]
        - (first_quat[3] * second_quat[1] - first_quat[1] * second_quat[3])
    )
    vector_three = (
        first_quat[0] * second_quat[3]
        + second_quat[0] * first_quat[3]
        - (first_quat[1] * second_quat[2] - first_quat[2] * second_quat[1])
    )
    return jnp.stack([scalar, vector_one, vector_two, vector_three])


def quat_conj(quaternion):
    return jnp.concatenate([quaternion[:1], -quaternion[1:]], axis=0)


def relax_sites(field, kernel_sum):
    kernel_norm = jnp.sqrt(jnp.sum(kernel_sum * kernel_sum, axis=0))
    rotated = OMEGA * quat_product(quat_conj(kernel_sum), quat_conj(field))
    relaxed = jnp.concatenate(
        [rotated[:1] + (1.0 - OMEGA) * kernel_norm[None], rotated[1:]], axis=0
    )
    relaxed_norm = jnp.sqrt(jnp.sum(relaxed * relaxed, axis=0))
    return quat_product(relaxed, field) / jnp.maximum(relaxed_norm, 1.0)[None]


def site_parity(coord_x, coord_z):
    rows_y = jnp.arange(LY, dtype=jnp.int32)
    rows_t = jnp.arange(LT, dtype=jnp.int32)
    return (
        coord_x[:, None, None, None]
        + coord_z[None, :, None, None]
        + rows_y[None, None, :, None]
        + rows_t[None, None, None, :]
    ) % 2


def fourier_tables(length):
    indices = jnp.arange(length, dtype=jnp.int32)
    phases = indices[:, None] * indices[None, :] % length
    angles = phases.astype(jnp.float32) * (2.0 * math.pi / length)
    return (jnp.cos(angles), jnp.sin(angles))


def along_axis(spectrum, axis_number):
    cosine, sine_part = fourier_tables(spectrum.shape[axis_number])
    moved_last = jnp.moveaxis(spectrum, axis_number, -1)
    cos_term = jnp.matmul(moved_last, cosine, precision=lax.Precision.HIGHEST)
    sin_term = jnp.matmul(moved_last, sine_part, precision=lax.Precision.HIGHEST)
    rotated = jnp.stack([cos_term[0] + sin_term[1], cos_term[1] - sin_term[0]])
    return jnp.moveaxis(rotated, -1, axis_number)


def along_x(spectrum):
    return along_axis(spectrum, 2)


def along_z(spectrum):
    return along_axis(spectrum, 3)


def body(links, gauge):
    slab_x = gauge.shape[1]
    slab_z = gauge.shape[2]
    count_wide = lax.axis_size("wide")
    count_narrow = lax.axis_size("narrow")
    coord_x = lax.axis_index("wide") * slab_x + jnp.arange(slab_x, dtype=jnp.int32)
    coord_z = lax.axis_index("narrow") * slab_z + jnp.arange(slab_z, dtype=jnp.int32)
    link = links.reshape((4, 4, slab_x, slab_z, LY, LT))
    field = gauge.reshape((4, slab_x, slab_z, LY, LT))
    parity = site_parity(coord_x, coord_z)
    from_below_x = from_behind(link[:, 0, slab_x - 1 :], "wide", 1)
    from_below_z = from_behind(link[:, 2, :, slab_z - 1 :], "narrow", 1)
    behind_links = [
        jnp.concatenate([from_below_x, link[:, 0, : slab_x - 1]], axis=1),
        jnp.roll(link[:, 1], 1, axis=3),
        jnp.concatenate([from_below_z, link[:, 2, :, : slab_z - 1]], axis=2),
        jnp.roll(link[:, 3], 1, axis=4),
    ]
    for half_sweep in range(HALF_SWEEPS):
        update_side = half_sweep % 2
        padded = padded_2(field, (("wide", 1), ("narrow", 2)), 1)
        center = padded[:, 1:-1, 1:-1]
        ahead_list = [
            padded[:, 2:, 1:-1],
            jnp.roll(center, -1, axis=3),
            padded[:, 1:-1, 2:],
            jnp.roll(center, -1, axis=4),
        ]
        behind_list = [
            padded[:, :-2, 1:-1],
            jnp.roll(center, 1, axis=3),
            padded[:, 1:-1, :-2],
            jnp.roll(center, 1, axis=4),
        ]
        kernel_sum = jnp.zeros(field.shape, jnp.float32)
        for direction in range(4):
            kernel_sum = (
                kernel_sum
                + quat_product(link[:, direction], quat_conj(ahead_list[direction]))
                + quat_product(
                    quat_conj(behind_links[direction]), quat_conj(behind_list[direction])
                )
            )
        field = jnp.where((parity == update_side)[None], relax_sites(field, kernel_sum), field)
    next_x = from_behind(field[:, :1], "wide", -1)
    next_z = from_behind(field, "narrow", -1)
    forward_list = [
        jnp.concatenate([field[:, 1:], next_x], axis=1),
        jnp.roll(field, -1, axis=3),
        jnp.concatenate([field[:, :, 1:], next_z], axis=2),
        jnp.roll(field, -1, axis=4),
    ]
    pieces = []
    for direction in range(4):
        transformed = quat_product(
            quat_product(field, link[:, direction]), quat_conj(forward_list[direction])
        )
        pieces.append(transformed[1:])
    potential = jnp.stack(pieces, axis=1).reshape((12, slab_x, slab_z, LY, LT))
    cosine_t, sine_t = fourier_tables(LT)
    real_part = jnp.matmul(potential, cosine_t, precision=lax.Precision.HIGHEST)
    imag_part = -jnp.matmul(potential, sine_t, precision=lax.Precision.HIGHEST)
    spectrum = along_axis(jnp.stack([real_part, imag_part]), 4)
    spectrum = along_x(lax.all_to_all(spectrum, "wide", split_axis=4, concat_axis=2, tiled=True))
    spectrum = along_z(lax.all_to_all(spectrum, "narrow", split_axis=5, concat_axis=3, tiled=True))
    scale = float(count_wide * slab_x * count_narrow * slab_z * LY * LT) ** (-0.5)
    spectrum = spectrum * scale
    full_x = spectrum.shape[2]
    full_z = spectrum.shape[3]
    spectrum = jnp.transpose(spectrum, (0, 1, 4, 5, 2, 3))
    spectrum = spectrum.reshape((2, 12, spectrum.shape[2], spectrum.shape[3], full_x * full_z))
    return (spectrum, field.reshape((4, slab_x, slab_z, LY * LT)))


ROWS = 8
INNER = LY // ROWS
LANES = INNER * LT
COMPS = 12
VMEM_MIB = 62
MESH = pl.DeviceIdType.MESH


def split_pair(table):
    high = table.astype(jnp.bfloat16)
    low = (table - high.astype(np.float32)).astype(jnp.bfloat16)
    return np.stack([np.asarray(high), np.asarray(low)])


def make_tables(wide, narrow, slab_x):
    turn = 2.0 * np.pi
    per_kt = LT // narrow
    k0 = np.arange(ROWS)
    angle = turn * (np.outer(k0, k0) % ROWS) / ROWS
    first = np.zeros((2, 16, ROWS, COMPS, ROWS))
    for c in range(COMPS):
        first[0, c, :, c, :] = np.cos(angle)
        first[1, c, :, c, :] = -np.sin(angle)
    first = first.reshape(256, COMPS * ROWS)
    inner = np.repeat(np.arange(INNER), LT)
    angle = turn * np.outer(k0, inner) / LY
    twiddle = np.stack([np.cos(angle), np.sin(angle)])
    time = np.tile(np.arange(LT), INNER)
    kb = np.arange(wide)
    kt = np.arange(LT)
    part_b = np.exp(-1j * turn * (np.outer(kb, inner) % wide) / wide)
    part_t = np.exp(-1j * turn * (np.outer(kt, time) % LT) / LT)
    phase = (part_b[:, None, :] * part_t[None]).reshape(wide, narrow, per_kt, LANES)
    second = np.empty((wide, narrow, 2, per_kt, 2, LANES))
    second[:, :, 0, :, 0] = phase.real
    second[:, :, 0, :, 1] = -phase.imag
    second[:, :, 1, :, 0] = phase.imag
    second[:, :, 1, :, 1] = phase.real
    second = second.transpose(0, 2, 1, 3, 4, 5).reshape(wide * narrow * 2 * per_kt, 2 * LANES)
    nx = wide * slab_x
    kx = np.arange(nx)
    kz = np.arange(narrow)
    part_x = np.exp(-1j * turn * (np.outer(kx, kx) % nx) / nx).reshape(nx, wide, slab_x)
    part_z = np.exp(-1j * turn * (np.outer(kz, kz) % narrow) / narrow)
    phase = part_x[:, None, :, None, :] * part_z[None, :, None, :, None]
    phase = phase * float(nx * narrow * LY * LT) ** (-0.5)
    third = np.empty((2, nx, narrow, wide, narrow, slab_x, 2))
    third[0, ..., 0] = phase.real
    third[0, ..., 1] = -phase.imag
    third[1, ..., 0] = phase.imag
    third[1, ..., 1] = phase.real
    third = third.transpose(0, 1, 2, 5, 6, 3, 4).reshape(2 * nx * narrow, wide * narrow * slab_x * 2)
    f32 = np.float32
    return (
        split_pair(first.astype(f32)),
        twiddle.astype(f32),
        split_pair(second.astype(f32)),
        split_pair(third.astype(f32)),
    )


def qmul(a, b):
    return [
        a[0] * b[0] - a[1] * b[1] - a[2] * b[2] - a[3] * b[3],
        a[0] * b[1] + b[0] * a[1] - (a[2] * b[3] - a[3] * b[2]),
        a[0] * b[2] + b[0] * a[2] - (a[3] * b[1] - a[1] * b[3]),
        a[0] * b[3] + b[0] * a[3] - (a[1] * b[2] - a[2] * b[1]),
    ]


def qconj(a):
    return [a[0], -a[1], -a[2], -a[3]]


def qadd(a, b):
    return [p + q for p, q in zip(a, b)]


def qwhere(mask, a, b):
    return [jnp.where(mask, p, q) for p, q in zip(a, b)]


def qnorm(a):
    return jnp.sqrt(a[0] * a[0] + a[1] * a[1] + a[2] * a[2] + a[3] * a[3])


def halves(value):
    high = value.astype(jnp.bfloat16)
    return high, (value - high.astype(jnp.float32)).astype(jnp.bfloat16)


def dot3(pair_a, pair_b, dims):
    def one(a, b):
        return lax.dot_general(a, b, (dims, ((), ())), preferred_element_type=jnp.float32)

    return one(pair_a[0], pair_b[0]) + (one(pair_a[1], pair_b[0]) + one(pair_a[0], pair_b[1]))


def fused(
    wide, narrow,
    links_hbm, gauge_hbm, first_hbm, twiddle_hbm, second_hbm, third_hbm,
    out_ref, field_ref,
    links_ref, gauge_ref, first_ref, twiddle_ref, second_ref, third_ref,
    face_out, face_in, pot, outgoing, arrived,
    load_sem, face_send, face_recv, far_send, far_recv, own_sem,
):
    my_w = lax.axis_index("wide")
    my_n = lax.axis_index("narrow")
    per_kt = LT // narrow
    loads = [
        pltpu.make_async_copy(source, target, load_sem.at[i])
        for i, (source, target) in enumerate(
            [
                (links_hbm, links_ref),
                (gauge_hbm, gauge_ref),
                (first_hbm, first_ref),
                (twiddle_hbm, twiddle_ref),
                (third_hbm, third_ref),
                (second_hbm, second_ref),
            ]
        )
    ]
    for load in loads:
        load.start()

    barrier = pltpu.get_barrier_semaphore()
    for i in range(wide):
        for k in range(narrow):
            if i or k:
                peer = (lax.rem(my_w + i, wide), lax.rem(my_n + k, narrow))
                pl.semaphore_signal(barrier, inc=1, device_id=peer, device_id_type=MESH)

    lane = lax.broadcasted_iota(jnp.int32, (ROWS, LANES), 1)
    inner = jnp.zeros((ROWS, LANES), jnp.int32)
    for j in range(1, INNER):
        inner = inner + jnp.where(lane >= LT * j, 1, 0)
    time = lane - LT * inner
    even = ((my_n + inner + time) & 1) == 0
    odd = jnp.logical_not(even)
    first_t, last_t = time == 0, time == LT - 1
    first_j, last_j = inner == 0, inner == INNER - 1

    def ahead_t(v):
        return jnp.where(last_t, pltpu.roll(v, LT - 1, 1), pltpu.roll(v, LANES - 1, 1))

    def behind_t(v):
        return jnp.where(first_t, pltpu.roll(v, LANES - LT + 1, 1), pltpu.roll(v, 1, 1))

    def ahead_y(v):
        moved = pltpu.roll(v, LANES - LT, 1)
        return jnp.where(last_j, pltpu.roll(moved, ROWS - 1, 0), moved)

    def behind_y(v):
        moved = pltpu.roll(v, LT, 1)
        return jnp.where(first_j, pltpu.roll(moved, 1, 0), moved)

    def tile(ref, index):
        return jnp.concatenate(
            [ref[pl.ds(index * 24 + s, ROWS, stride=3), :] for s in range(3)], axis=1
        )

    def both(ref, index_zero):
        zero, one = tile(ref, index_zero), tile(ref, index_zero + 1)
        return jnp.where(even, zero, one), jnp.where(even, one, zero)

    loads[0].wait()
    loads[1].wait()
    link = [[None] * 4, [None] * 4]
    for mu in range(4):
        pairs = [both(links_ref, (a * 4 + mu) * 2) for a in range(4)]
        for p in range(2):
            link[p][mu] = [pair[p] for pair in pairs]
    pairs = [both(gauge_ref, a * 2) for a in range(4)]
    field = [[pair[p] for pair in pairs] for p in range(2)]

    def neighbour(step_w, step_n):
        return (
            lax.rem(my_w + step_w + wide, wide),
            lax.rem(my_n + step_n + narrow, narrow),
        )

    def send_face(source, slot, step_w, step_n, parts):
        copy = pltpu.make_async_remote_copy(
            src_ref=face_out.at[source, pl.ds(0, parts)],
            dst_ref=face_in.at[slot, pl.ds(0, parts)],
            send_sem=face_send.at[slot],
            recv_sem=face_recv.at[slot],
            device_id=neighbour(step_w, step_n),
            device_id_type=MESH,
        )
        copy.start()
        return copy

    def put_face(source, value):
        for a in range(4):
            face_out[source, a] = value[a]

    def got_face(slot):
        return [face_in[slot, a] for a in range(4)]

    def put_packed(source, value, lanes):
        for a in range(2):
            face_out[source, a] = jnp.where(lanes, value[2 * a], behind_t(value[2 * a + 1]))

    def got_packed(slot):
        pairs = [face_in[slot, a] for a in range(2)]
        return [v for pair in pairs for v in (pair, ahead_t(pair))]

    copies = []
    moved_links = None
    kept_x = kept_z = None
    for half in range(HALF_SWEEPS):
        p = half % 2
        here = even if p == 0 else odd
        other = field[1 - p]
        away = odd if p == 0 else even
        source, slot = 4 * half, 4 * half
        put_packed(source, other, away)
        moved_x = qmul(other, link[1 - p][0])
        put_packed(source + 1, moved_x, here)
        put_face(source + 2, other)
        if half == 0:
            pl.semaphore_wait(barrier, wide * narrow - 1)
        started = [
            send_face(source, slot, -1, 0, 2),
            send_face(source + 1, slot + 2, 1, 0, 2),
            send_face(source + 2, slot + 1, 0, -1, 4),
        ]
        moved_z = qmul(other, link[1 - p][2])
        put_face(source + 3, moved_z)
        started.append(send_face(source + 3, slot + 3, 0, 1, 4))
        moved_links = [
            moved_x, qmul(other, link[1 - p][1]), moved_z, qmul(other, link[1 - p][3])
        ]
        copies += started
        total = qmul([ahead_y(v) for v in other], qconj(link[p][1]))
        total = qadd(total, [behind_y(v) for v in moved_links[1]])
        total = qadd(total, qmul([ahead_t(v) for v in other], qconj(link[p][3])))
        total = qadd(total, [behind_t(v) for v in moved_links[3]])
        started[2].wait_recv()
        kept_z = got_face(slot + 1)
        total = qadd(total, qmul(kept_z, qconj(link[p][2])))
        started[3].wait_recv()
        total = qadd(total, got_face(slot + 3))
        started[0].wait_recv()
        kept_x = got_packed(slot)
        total = qadd(total, qmul(qwhere(here, other, kept_x), qconj(link[p][0])))
        started[1].wait_recv()
        total = qadd(total, qwhere(here, got_packed(slot + 2), moved_links[0]))
        centre = field[p]
        relaxed = [OMEGA * v for v in qmul(total, qconj(centre))]
        relaxed[0] = relaxed[0] + (1.0 - OMEGA) * qnorm(total)
        bound = jnp.maximum(qnorm(relaxed), 1.0)
        field[p] = [v / bound for v in qmul(relaxed, centre)]

    p = (HALF_SWEEPS - 1) % 2
    here = even if p == 0 else odd
    source, slot = 4 * HALF_SWEEPS, 4 * HALF_SWEEPS
    put_packed(source, field[p], here)
    put_face(source + 1, field[p])
    started = [send_face(source, slot, -1, 0, 2), send_face(source + 1, slot + 1, 0, -1, 4)]
    copies += started
    for a in range(4):
        zero = jnp.where(even, field[0][a], field[1][a])
        one = jnp.where(even, field[1][a], field[0][a])
        for x, value in enumerate((zero, one)):
            for s in range(3):
                field_ref[pl.ds((a * 2 + x) * 24 + s, ROWS, stride=3), :] = value[
                    :, 128 * s : 128 * (s + 1)
                ]
    carried = [None, None]
    carried[1 - p] = moved_links
    carried[p] = [qmul(field[p], link[p][mu]) for mu in range(4)]

    def put_potential(mu, ahead):
        value = [qmul(carried[q][mu], qconj(ahead[q])) for q in range(2)]
        for a in range(3):
            c = 4 * a + mu
            zero = jnp.where(even, value[0][a + 1], value[1][a + 1])
            one = jnp.where(even, value[1][a + 1], value[0][a + 1])
            pot[0, c * ROWS : (c + 1) * ROWS, :] = zero
            pot[1, c * ROWS : (c + 1) * ROWS, :] = one

    put_potential(1, [[ahead_y(v) for v in field[1 - q]] for q in range(2)])
    put_potential(3, [[ahead_t(v) for v in field[1 - q]] for q in range(2)])
    started[1].wait_recv()
    fresh_z = got_face(slot + 1)
    put_potential(2, [[kept_z, fresh_z][q != p] for q in range(2)])
    started[0].wait_recv()
    fresh_x = got_packed(slot)
    there = odd if p == 0 else even
    ahead = [None, None]
    ahead[p] = qwhere(here, field[1 - p], kept_x)
    ahead[1 - p] = qwhere(there, field[p], fresh_x)
    put_potential(0, ahead)

    loads[2].wait()
    loads[3].wait()
    first = (first_ref[0], first_ref[1])
    cosine, sine = twiddle_ref[0][None], twiddle_ref[1][None]
    highs, lows = [], []
    for x in range(2):
        turned_r = dot3(first, halves(pot[x]), ((1,), (0,))).reshape(2, 16, ROWS, LANES)
        real = turned_r[0] * cosine + turned_r[1] * sine
        imag = turned_r[1] * cosine - turned_r[0] * sine
        both_parts = jnp.concatenate(
            [real.reshape(128, LANES), imag.reshape(128, LANES)], axis=1
        )
        high, low = halves(both_parts)
        highs.append(high)
        lows.append(low)
    used = COMPS * ROWS
    over = 128 - used

    def arrange(parts):
        zeros = jnp.zeros((over, 2 * LANES), jnp.bfloat16)
        return jnp.concatenate(
            [parts[0][:used], parts[1][:over], zeros, parts[1][over:used], zeros], axis=0
        )

    mid = (arrange(highs), arrange(lows))
    loads[5].wait()
    per_b = narrow * per_kt
    pair = 2
    groups = wide // pair
    block = message_rows(per_kt)
    my_z, my_x = my_w // pair, lax.rem(my_w, pair)

    def span(w, n):
        return pl.ds(pl.multiple_of((w * narrow + n) * block, 8), block)

    mine = span(my_w, my_n)
    steps = sorted(range(groups), key=lambda step: -min(step, groups - step))
    own = None
    for place, step in enumerate(steps):
        group = lax.rem(my_z + step, groups)
        rows = pl.ds(pl.multiple_of(group * (pair * 2 * per_b), 16), pair * 2 * per_b)
        value = dot3((second_ref[0, rows, :], second_ref[1, rows, :]), mid, ((1,), (1,)))
        for q in range(pair):
            real = value[q * 2 * per_b : q * 2 * per_b + per_b]
            imag = value[q * 2 * per_b + per_b : (q + 1) * 2 * per_b]
            extra = real[:, 128:] + pltpu.roll(imag[:, 128:], 64, 1)
            for n in range(narrow):
                base = ((place * pair + q) * narrow + n) * block
                take = slice(n * per_kt, (n + 1) * per_kt)
                outgoing[base : base + per_kt, :] = real[take, :128]
                outgoing[base + per_kt : base + 2 * per_kt, :] = imag[take, :128]
                outgoing[base + 2 * per_kt : base + 3 * per_kt, :] = extra[take]
                outgoing[base + 3 * per_kt : base + block, :] = jnp.zeros(
                    (block - 3 * per_kt, 128), jnp.float32
                )
        for q in range(pair):
            x = lax.rem(my_x + q, pair)
            for k in range(narrow):
                w, n = group * pair + x, lax.rem(my_n + k, narrow)
                index = (step * pair + q) * narrow + k
                held = pl.ds(
                    pl.multiple_of(((place * pair + x) * narrow + n) * block, 8), block
                )
                if index == 0:
                    own = pltpu.make_async_copy(outgoing.at[held], arrived.at[mine], own_sem)
                    own.start()
                    continue
                copy = pltpu.make_async_remote_copy(
                    src_ref=outgoing.at[held],
                    dst_ref=arrived.at[mine],
                    send_sem=far_send.at[index],
                    recv_sem=far_recv.at[index],
                    device_id=(w, n),
                    device_id_type=MESH,
                )
                copy.start()
                copies.append(copy)
    own.wait()
    loads[4].wait()
    for step in range(groups):
        for q in range(pair):
            for k in range(narrow):
                index = (step * pair + q) * narrow + k
                if index == 0:
                    continue
                w = lax.rem(my_z + groups - step, groups) * pair + lax.rem(my_x + q, pair)
                n = lax.rem(my_n + narrow - k, narrow)
                pltpu.make_async_remote_copy(
                    src_ref=outgoing.at[pl.ds(0, block)],
                    dst_ref=arrived.at[span(w, n)],
                    send_sem=far_send.at[index],
                    recv_sem=far_recv.at[index],
                    device_id=(w, n),
                    device_id_type=MESH,
                ).wait_recv()

    third = (third_ref[0], third_ref[1])
    devices = wide * narrow
    momenta = third_ref.shape[1] // 2
    start = lax.broadcasted_iota(jnp.int32, (devices, 128), 1) < over
    for kt in range(0, per_kt, 2):
        columns = []
        for m in range(2):
            real, imag, extra = [
                arrived[pl.ds(part * per_kt + kt + m, devices, stride=block), :]
                for part in range(3)
            ]
            real_one = jnp.where(start, pltpu.roll(real, over, 1), extra)
            imag_one = jnp.where(start, pltpu.roll(imag, over, 1), pltpu.roll(extra, 64, 1))
            columns.append(jnp.concatenate([real, imag, real_one, imag_one], axis=0))
        value = dot3(third, halves(jnp.concatenate(columns, axis=1)), ((1,), (0,)))
        for m in range(2):
            whole = value[:, 128 * m : 128 * (m + 1)].T[:used]
            out_ref[0, :, kt + m] = whole[:, :momenta].reshape(COMPS, ROWS, momenta)
            out_ref[1, :, kt + m] = whole[:, momenta:].reshape(COMPS, ROWS, momenta)
    for copy in copies:
        copy.wait_send()


def message_rows(per_kt):
    return -(-3 * per_kt // 8) * 8


def fused_body(wide, narrow, links, gauge):
    slab_x = gauge.shape[1]
    tables = make_tables(wide, narrow, slab_x)
    devices = wide * narrow
    per_kt = LT // narrow
    block = message_rows(per_kt)
    faces = 4 * HALF_SWEEPS + 2
    vmem = pl.BlockSpec(memory_space=pltpu.VMEM)
    operands = [
        links.reshape(4 * 4 * slab_x * 24, 128),
        gauge.reshape(4 * slab_x * 24, 128),
        *[jnp.asarray(table) for table in tables],
    ]
    spectrum, field = pl.pallas_call(
        lambda *refs: fused(wide, narrow, *refs),
        out_shape=(
            jax.ShapeDtypeStruct((2, COMPS, per_kt, ROWS, wide * slab_x * narrow), jnp.float32),
            jax.ShapeDtypeStruct((4 * slab_x * 24, 128), jnp.float32),
        ),
        in_specs=[pl.BlockSpec(memory_space=pl.ANY)] * len(operands),
        out_specs=(vmem, vmem),
        scratch_shapes=[
            *[pltpu.VMEM(value.shape, value.dtype) for value in operands],
            pltpu.VMEM((faces, 4, ROWS, LANES), jnp.float32),
            pltpu.VMEM((faces, 4, ROWS, LANES), jnp.float32),
            pltpu.VMEM((2, COMPS * ROWS, LANES), jnp.float32),
            pltpu.VMEM((devices * block, 128), jnp.float32),
            pltpu.VMEM((devices * block, 128), jnp.float32),
            pltpu.SemaphoreType.DMA((len(operands),)),
            pltpu.SemaphoreType.DMA((faces,)),
            pltpu.SemaphoreType.DMA((faces,)),
            pltpu.SemaphoreType.DMA((devices,)),
            pltpu.SemaphoreType.DMA((devices,)),
            pltpu.SemaphoreType.DMA,
        ],
        compiler_params=pltpu.CompilerParams(
            collective_id=0, has_side_effects=True, vmem_limit_bytes=VMEM_MIB * 1024 * 1024
        ),
    )(*operands)
    spectrum = jnp.transpose(spectrum, (0, 1, 3, 2, 4))
    return spectrum, field.reshape(gauge.shape)


def solution(mesh):
    in_specs = (P(None, None, "wide", "narrow", None), P(None, "wide", "narrow", None))
    out_specs = (P(None, None, "wide", "narrow", None), P(None, "wide", "narrow", None))
    wide, narrow = mesh.shape["wide"], mesh.shape["narrow"]

    def per_device(links, gauge):
        slab_x, slab_z = gauge.shape[1:3]
        fits = slab_x == 2 and slab_z == 1 and wide * ROWS == LY and wide * narrow * 4 == 128
        if fits:
            return fused_body(wide, narrow, links, gauge)
        return body(links, gauge)

    return jax.shard_map(
        per_device, mesh=mesh, in_specs=in_specs, out_specs=out_specs, check_vma=False
    )
```

```python
import math

import jax
import jax.numpy as jnp
import numpy as np
from jax import lax
from jax.experimental import pallas as pl
from jax.experimental.pallas import tpu as pltpu
from jax.sharding import PartitionSpec as P

LY = 64
LT = 48
HALF_SWEEPS = 2


OMEGA = 1.7


def from_behind(value, axis, steps):
    count = lax.axis_size(axis)
    pairs = [(source, (source + steps) % count) for source in range(count)]
    return lax.ppermute(value, axis, pairs)


def padded_2(block, sides, width):
    for axis, dim in sides:
        count = lax.axis_size(axis)
        forward = [(i, i + 1) for i in range(count - 1)]
        forward.append((count - 1, 0))
        backward = [(target, source) for source, target in forward]
        low = lax.ppermute(
            lax.slice_in_dim(block, block.shape[dim] - width, None, axis=dim), axis, forward
        )
        high = lax.ppermute(lax.slice_in_dim(block, 0, width, axis=dim), axis, backward)
        block = jnp.concatenate([low, block, high], axis=dim)
    return block


def quat_product(first_quat, second_quat):
    scalar = (
        first_quat[0] * second_quat[0]
        - first_quat[1] * second_quat[1]
        - first_quat[2] * second_quat[2]
        - first_quat[3] * second_quat[3]
    )
    vector_one = (
        first_quat[0] * second_quat[1]
        + second_quat[0] * first_quat[1]
        - (first_quat[2] * second_quat[3] - first_quat[3] * second_quat[2])
    )
    vector_two = (
        first_quat[0] * second_quat[2]
        + second_quat[0] * first_quat[2]
        - (first_quat[3] * second_quat[1] - first_quat[1] * second_quat[3])
    )
    vector_three = (
        first_quat[0] * second_quat[3]
        + second_quat[0] * first_quat[3]
        - (first_quat[1] * second_quat[2] - first_quat[2] * second_quat[1])
    )
    return jnp.stack([scalar, vector_one, vector_two, vector_three])


def quat_conj(quaternion):
    return jnp.concatenate([quaternion[:1], -quaternion[1:]], axis=0)


def relax_sites(field, kernel_sum):
    kernel_norm = jnp.sqrt(jnp.sum(kernel_sum * kernel_sum, axis=0))
    rotated = OMEGA * quat_product(quat_conj(kernel_sum), quat_conj(field))
    relaxed = jnp.concatenate(
        [rotated[:1] + (1.0 - OMEGA) * kernel_norm[None], rotated[1:]], axis=0
    )
    relaxed_norm = jnp.sqrt(jnp.sum(relaxed * relaxed, axis=0))
    return quat_product(relaxed, field) / jnp.maximum(relaxed_norm, 1.0)[None]


def site_parity(coord_x, coord_z):
    rows_y = jnp.arange(LY, dtype=jnp.int32)
    rows_t = jnp.arange(LT, dtype=jnp.int32)
    return (
        coord_x[:, None, None, None]
        + coord_z[None, :, None, None]
        + rows_y[None, None, :, None]
        + rows_t[None, None, None, :]
    ) % 2


def fourier_tables(length):
    indices = jnp.arange(length, dtype=jnp.int32)
    phases = indices[:, None] * indices[None, :] % length
    angles = phases.astype(jnp.float32) * (2.0 * math.pi / length)
    return (jnp.cos(angles), jnp.sin(angles))


def along_axis(spectrum, axis_number):
    cosine, sine_part = fourier_tables(spectrum.shape[axis_number])
    moved_last = jnp.moveaxis(spectrum, axis_number, -1)
    cos_term = jnp.matmul(moved_last, cosine, precision=lax.Precision.HIGHEST)
    sin_term = jnp.matmul(moved_last, sine_part, precision=lax.Precision.HIGHEST)
    rotated = jnp.stack([cos_term[0] + sin_term[1], cos_term[1] - sin_term[0]])
    return jnp.moveaxis(rotated, -1, axis_number)


def along_x(spectrum):
    return along_axis(spectrum, 2)


def along_z(spectrum):
    return along_axis(spectrum, 3)


def body(links, gauge):
    slab_x = gauge.shape[1]
    slab_z = gauge.shape[2]
    count_wide = lax.axis_size("wide")
    count_narrow = lax.axis_size("narrow")
    coord_x = lax.axis_index("wide") * slab_x + jnp.arange(slab_x, dtype=jnp.int32)
    coord_z = lax.axis_index("narrow") * slab_z + jnp.arange(slab_z, dtype=jnp.int32)
    link = links.reshape((4, 4, slab_x, slab_z, LY, LT))
    field = gauge.reshape((4, slab_x, slab_z, LY, LT))
    parity = site_parity(coord_x, coord_z)
    from_below_x = from_behind(link[:, 0, slab_x - 1 :], "wide", 1)
    from_below_z = from_behind(link[:, 2, :, slab_z - 1 :], "narrow", 1)
    behind_links = [
        jnp.concatenate([from_below_x, link[:, 0, : slab_x - 1]], axis=1),
        jnp.roll(link[:, 1], 1, axis=3),
        jnp.concatenate([from_below_z, link[:, 2, :, : slab_z - 1]], axis=2),
        jnp.roll(link[:, 3], 1, axis=4),
    ]
    for half_sweep in range(HALF_SWEEPS):
        update_side = half_sweep % 2
        padded = padded_2(field, (("wide", 1), ("narrow", 2)), 1)
        center = padded[:, 1:-1, 1:-1]
        ahead_list = [
            padded[:, 2:, 1:-1],
            jnp.roll(center, -1, axis=3),
            padded[:, 1:-1, 2:],
            jnp.roll(center, -1, axis=4),
        ]
        behind_list = [
            padded[:, :-2, 1:-1],
            jnp.roll(center, 1, axis=3),
            padded[:, 1:-1, :-2],
            jnp.roll(center, 1, axis=4),
        ]
        kernel_sum = jnp.zeros(field.shape, jnp.float32)
        for direction in range(4):
            kernel_sum = (
                kernel_sum
                + quat_product(link[:, direction], quat_conj(ahead_list[direction]))
                + quat_product(
                    quat_conj(behind_links[direction]), quat_conj(behind_list[direction])
                )
            )
        field = jnp.where((parity == update_side)[None], relax_sites(field, kernel_sum), field)
    next_x = from_behind(field[:, :1], "wide", -1)
    next_z = from_behind(field, "narrow", -1)
    forward_list = [
        jnp.concatenate([field[:, 1:], next_x], axis=1),
        jnp.roll(field, -1, axis=3),
        jnp.concatenate([field[:, :, 1:], next_z], axis=2),
        jnp.roll(field, -1, axis=4),
    ]
    pieces = []
    for direction in range(4):
        transformed = quat_product(
            quat_product(field, link[:, direction]), quat_conj(forward_list[direction])
        )
        pieces.append(transformed[1:])
    potential = jnp.stack(pieces, axis=1).reshape((12, slab_x, slab_z, LY, LT))
    cosine_t, sine_t = fourier_tables(LT)
    real_part = jnp.matmul(potential, cosine_t, precision=lax.Precision.HIGHEST)
    imag_part = -jnp.matmul(potential, sine_t, precision=lax.Precision.HIGHEST)
    spectrum = along_axis(jnp.stack([real_part, imag_part]), 4)
    spectrum = along_x(lax.all_to_all(spectrum, "wide", split_axis=4, concat_axis=2, tiled=True))
    spectrum = along_z(lax.all_to_all(spectrum, "narrow", split_axis=5, concat_axis=3, tiled=True))
    scale = float(count_wide * slab_x * count_narrow * slab_z * LY * LT) ** (-0.5)
    spectrum = spectrum * scale
    full_x = spectrum.shape[2]
    full_z = spectrum.shape[3]
    spectrum = jnp.transpose(spectrum, (0, 1, 4, 5, 2, 3))
    spectrum = spectrum.reshape((2, 12, spectrum.shape[2], spectrum.shape[3], full_x * full_z))
    return (spectrum, field.reshape((4, slab_x, slab_z, LY * LT)))


ROWS = 8
INNER = LY // ROWS
LANES = INNER * LT
COMPS = 12
VMEM_MIB = 62
MESH = pl.DeviceIdType.MESH


def split_pair(table):
    high = table.astype(jnp.bfloat16)
    low = (table - high.astype(np.float32)).astype(jnp.bfloat16)
    return np.stack([np.asarray(high), np.asarray(low)])


def make_tables(wide, narrow, slab_x):
    turn = 2.0 * np.pi
    per_kt = LT // narrow
    k0 = np.arange(ROWS)
    angle = turn * (np.outer(k0, k0) % ROWS) / ROWS
    first = np.zeros((2, 16, ROWS, COMPS, ROWS))
    for c in range(COMPS):
        first[0, c, :, c, :] = np.cos(angle)
        first[1, c, :, c, :] = -np.sin(angle)
    first = first.reshape(256, COMPS * ROWS)
    inner = np.repeat(np.arange(INNER), LT)
    angle = turn * np.outer(k0, inner) / LY
    twiddle = np.stack([np.cos(angle), np.sin(angle)])
    time = np.tile(np.arange(LT), INNER)
    kb = np.arange(wide)
    kt = np.arange(LT)
    part_b = np.exp(-1j * turn * (np.outer(kb, inner) % wide) / wide)
    part_t = np.exp(-1j * turn * (np.outer(kt, time) % LT) / LT)
    phase = (part_b[:, None, :] * part_t[None]).reshape(wide, narrow, per_kt, LANES)
    second = np.empty((wide, narrow, 2, per_kt, 2, LANES))
    second[:, :, 0, :, 0] = phase.real
    second[:, :, 0, :, 1] = -phase.imag
    second[:, :, 1, :, 0] = phase.imag
    second[:, :, 1, :, 1] = phase.real
    second = second.transpose(0, 2, 1, 3, 4, 5).reshape(wide * narrow * 2 * per_kt, 2 * LANES)
    nx = wide * slab_x
    kx = np.arange(nx)
    kz = np.arange(narrow)
    part_x = np.exp(-1j * turn * (np.outer(kx, kx) % nx) / nx).reshape(nx, wide, slab_x)
    part_z = np.exp(-1j * turn * (np.outer(kz, kz) % narrow) / narrow)
    phase = part_x[:, None, :, None, :] * part_z[None, :, None, :, None]
    phase = phase * float(nx * narrow * LY * LT) ** (-0.5)
    third = np.empty((2, nx, narrow, wide, narrow, slab_x, 2))
    third[0, ..., 0] = phase.real
    third[0, ..., 1] = -phase.imag
    third[1, ..., 0] = phase.imag
    third[1, ..., 1] = phase.real
    third = third.transpose(0, 1, 2, 5, 6, 3, 4).reshape(2 * nx * narrow, wide * narrow * slab_x * 2)
    f32 = np.float32
    return (
        split_pair(first.astype(f32)),
        twiddle.astype(f32),
        split_pair(second.astype(f32)),
        split_pair(third.astype(f32)),
    )


def qmul(a, b):
    return [
        a[0] * b[0] - a[1] * b[1] - a[2] * b[2] - a[3] * b[3],
        a[0] * b[1] + b[0] * a[1] - (a[2] * b[3] - a[3] * b[2]),
        a[0] * b[2] + b[0] * a[2] - (a[3] * b[1] - a[1] * b[3]),
        a[0] * b[3] + b[0] * a[3] - (a[1] * b[2] - a[2] * b[1]),
    ]


def qconj(a):
    return [a[0], -a[1], -a[2], -a[3]]


def qadd(a, b):
    return [p + q for p, q in zip(a, b)]


def qwhere(mask, a, b):
    return [jnp.where(mask, p, q) for p, q in zip(a, b)]


def qnorm(a):
    return jnp.sqrt(a[0] * a[0] + a[1] * a[1] + a[2] * a[2] + a[3] * a[3])


def halves(value):
    high = value.astype(jnp.bfloat16)
    return high, (value - high.astype(jnp.float32)).astype(jnp.bfloat16)


def dot3(pair_a, pair_b, dims):
    def one(a, b):
        return lax.dot_general(a, b, (dims, ((), ())), preferred_element_type=jnp.float32)

    return one(pair_a[0], pair_b[0]) + (one(pair_a[1], pair_b[0]) + one(pair_a[0], pair_b[1]))


def fused(
    wide, narrow,
    links_hbm, gauge_hbm, first_hbm, twiddle_hbm, second_hbm, third_hbm,
    out_ref, field_ref,
    links_ref, gauge_ref, first_ref, twiddle_ref, second_ref, third_ref,
    face_out, face_in, pot, outgoing, arrived,
    load_sem, face_send, face_recv, far_send, far_recv, own_sem,
):
    my_w = lax.axis_index("wide")
    my_n = lax.axis_index("narrow")
    per_kt = LT // narrow
    loads = [
        pltpu.make_async_copy(source, target, load_sem.at[i])
        for i, (source, target) in enumerate(
            [
                (links_hbm, links_ref),
                (gauge_hbm, gauge_ref),
                (first_hbm, first_ref),
                (twiddle_hbm, twiddle_ref),
                (third_hbm, third_ref),
                (second_hbm, second_ref),
            ]
        )
    ]
    for load in loads:
        load.start()

    barrier = pltpu.get_barrier_semaphore()
    for i in range(wide):
        for k in range(narrow):
            if i or k:
                peer = (lax.rem(my_w + i, wide), lax.rem(my_n + k, narrow))
                pl.semaphore_signal(barrier, inc=1, device_id=peer, device_id_type=MESH)

    lane = lax.broadcasted_iota(jnp.int32, (ROWS, LANES), 1)
    inner = jnp.zeros((ROWS, LANES), jnp.int32)
    for j in range(1, INNER):
        inner = inner + jnp.where(lane >= LT * j, 1, 0)
    time = lane - LT * inner
    even = ((my_n + inner + time) & 1) == 0
    odd = jnp.logical_not(even)
    first_t, last_t = time == 0, time == LT - 1
    first_j, last_j = inner == 0, inner == INNER - 1

    def ahead_t(v):
        return jnp.where(last_t, pltpu.roll(v, LT - 1, 1), pltpu.roll(v, LANES - 1, 1))

    def behind_t(v):
        return jnp.where(first_t, pltpu.roll(v, LANES - LT + 1, 1), pltpu.roll(v, 1, 1))

    def ahead_y(v):
        moved = pltpu.roll(v, LANES - LT, 1)
        return jnp.where(last_j, pltpu.roll(moved, ROWS - 1, 0), moved)

    def behind_y(v):
        moved = pltpu.roll(v, LT, 1)
        return jnp.where(first_j, pltpu.roll(moved, 1, 0), moved)

    def tile(ref, index):
        return jnp.concatenate(
            [ref[pl.ds(index * 24 + s, ROWS, stride=3), :] for s in range(3)], axis=1
        )

    def both(ref, index_zero):
        zero, one = tile(ref, index_zero), tile(ref, index_zero + 1)
        return jnp.where(even, zero, one), jnp.where(even, one, zero)

    loads[0].wait()
    loads[1].wait()
    link = [[None] * 4, [None] * 4]
    for mu in range(4):
        pairs = [both(links_ref, (a * 4 + mu) * 2) for a in range(4)]
        for p in range(2):
            link[p][mu] = [pair[p] for pair in pairs]
    pairs = [both(gauge_ref, a * 2) for a in range(4)]
    field = [[pair[p] for pair in pairs] for p in range(2)]

    def neighbour(step_w, step_n):
        return (
            lax.rem(my_w + step_w + wide, wide),
            lax.rem(my_n + step_n + narrow, narrow),
        )

    def send_face(source, slot, step_w, step_n, parts):
        copy = pltpu.make_async_remote_copy(
            src_ref=face_out.at[source, pl.ds(0, parts)],
            dst_ref=face_in.at[slot, pl.ds(0, parts)],
            send_sem=face_send.at[slot],
            recv_sem=face_recv.at[slot],
            device_id=neighbour(step_w, step_n),
            device_id_type=MESH,
        )
        copy.start()
        return copy

    def put_face(source, value):
        for a in range(4):
            face_out[source, a] = value[a]

    def got_face(slot):
        return [face_in[slot, a] for a in range(4)]

    def put_packed(source, value, lanes):
        for a in range(2):
            face_out[source, a] = jnp.where(lanes, value[2 * a], behind_t(value[2 * a + 1]))

    def got_packed(slot):
        pairs = [face_in[slot, a] for a in range(2)]
        return [v for pair in pairs for v in (pair, ahead_t(pair))]

    copies = []
    moved_links = None
    kept_x = kept_z = None
    for half in range(HALF_SWEEPS):
        p = half % 2
        here = even if p == 0 else odd
        other = field[1 - p]
        away = odd if p == 0 else even
        source, slot = 4 * half, 4 * half
        put_packed(source, other, away)
        moved_x = qmul(other, link[1 - p][0])
        put_packed(source + 1, moved_x, here)
        put_face(source + 2, other)
        if half == 0:
            pl.semaphore_wait(barrier, wide * narrow - 1)
        started = [
            send_face(source, slot, -1, 0, 2),
            send_face(source + 1, slot + 2, 1, 0, 2),
            send_face(source + 2, slot + 1, 0, -1, 4),
        ]
        moved_z = qmul(other, link[1 - p][2])
        put_face(source + 3, moved_z)
        started.append(send_face(source + 3, slot + 3, 0, 1, 4))
        moved_links = [
            moved_x, qmul(other, link[1 - p][1]), moved_z, qmul(other, link[1 - p][3])
        ]
        copies += started
        total = qmul([ahead_y(v) for v in other], qconj(link[p][1]))
        total = qadd(total, [behind_y(v) for v in moved_links[1]])
        total = qadd(total, qmul([ahead_t(v) for v in other], qconj(link[p][3])))
        total = qadd(total, [behind_t(v) for v in moved_links[3]])
        started[2].wait_recv()
        kept_z = got_face(slot + 1)
        total = qadd(total, qmul(kept_z, qconj(link[p][2])))
        started[3].wait_recv()
        total = qadd(total, got_face(slot + 3))
        started[0].wait_recv()
        kept_x = got_packed(slot)
        total = qadd(total, qmul(qwhere(here, other, kept_x), qconj(link[p][0])))
        started[1].wait_recv()
        total = qadd(total, qwhere(here, got_packed(slot + 2), moved_links[0]))
        centre = field[p]
        relaxed = [OMEGA * v for v in qmul(total, qconj(centre))]
        relaxed[0] = relaxed[0] + (1.0 - OMEGA) * qnorm(total)
        bound = jnp.maximum(qnorm(relaxed), 1.0)
        field[p] = [v / bound for v in qmul(relaxed, centre)]

    p = (HALF_SWEEPS - 1) % 2
    here = even if p == 0 else odd
    source, slot = 4 * HALF_SWEEPS, 4 * HALF_SWEEPS
    put_packed(source, field[p], here)
    put_face(source + 1, field[p])
    started = [send_face(source, slot, -1, 0, 2), send_face(source + 1, slot + 1, 0, -1, 4)]
    copies += started
    for a in range(4):
        zero = jnp.where(even, field[0][a], field[1][a])
        one = jnp.where(even, field[1][a], field[0][a])
        for x, value in enumerate((zero, one)):
            for s in range(3):
                field_ref[pl.ds((a * 2 + x) * 24 + s, ROWS, stride=3), :] = value[
                    :, 128 * s : 128 * (s + 1)
                ]
    carried = [None, None]
    carried[1 - p] = moved_links
    carried[p] = [qmul(field[p], link[p][mu]) for mu in range(4)]

    def put_potential(mu, ahead):
        value = [qmul(carried[q][mu], qconj(ahead[q])) for q in range(2)]
        for a in range(3):
            c = 4 * a + mu
            zero = jnp.where(even, value[0][a + 1], value[1][a + 1])
            one = jnp.where(even, value[1][a + 1], value[0][a + 1])
            pot[0, c * ROWS : (c + 1) * ROWS, :] = zero
            pot[1, c * ROWS : (c + 1) * ROWS, :] = one

    put_potential(1, [[ahead_y(v) for v in field[1 - q]] for q in range(2)])
    put_potential(3, [[ahead_t(v) for v in field[1 - q]] for q in range(2)])
    started[1].wait_recv()
    fresh_z = got_face(slot + 1)
    put_potential(2, [[kept_z, fresh_z][q != p] for q in range(2)])
    started[0].wait_recv()
    fresh_x = got_packed(slot)
    there = odd if p == 0 else even
    ahead = [None, None]
    ahead[p] = qwhere(here, field[1 - p], kept_x)
    ahead[1 - p] = qwhere(there, field[p], fresh_x)
    put_potential(0, ahead)

    loads[2].wait()
    loads[3].wait()
    first = (first_ref[0], first_ref[1])
    cosine, sine = twiddle_ref[0][None], twiddle_ref[1][None]
    highs, lows = [], []
    for x in range(2):
        turned_r = dot3(first, halves(pot[x]), ((1,), (0,))).reshape(2, 16, ROWS, LANES)
        real = turned_r[0] * cosine + turned_r[1] * sine
        imag = turned_r[1] * cosine - turned_r[0] * sine
        both_parts = jnp.concatenate(
            [real.reshape(128, LANES), imag.reshape(128, LANES)], axis=1
        )
        high, low = halves(both_parts)
        highs.append(high)
        lows.append(low)
    used = COMPS * ROWS
    over = 128 - used

    def arrange(parts):
        zeros = jnp.zeros((over, 2 * LANES), jnp.bfloat16)
        return jnp.concatenate(
            [parts[0][:used], parts[1][:over], zeros, parts[1][over:used], zeros], axis=0
        )

    mid = (arrange(highs), arrange(lows))
    loads[5].wait()
    per_b = narrow * per_kt
    pair = 2
    groups = wide // pair
    block = message_rows(per_kt)
    my_z, my_x = my_w // pair, lax.rem(my_w, pair)

    def span(w, n):
        return pl.ds(pl.multiple_of((w * narrow + n) * block, 8), 3 * per_kt)

    mine = span(my_w, my_n)
    steps = sorted(range(groups), key=lambda step: -min(step, groups - step))
    own = None
    for place, step in enumerate(steps):
        group = lax.rem(my_z + step, groups)
        rows = pl.ds(pl.multiple_of(group * (pair * 2 * per_b), 16), pair * 2 * per_b)
        value = dot3((second_ref[0, rows, :], second_ref[1, rows, :]), mid, ((1,), (1,)))
        for q in range(pair):
            real = value[q * 2 * per_b : q * 2 * per_b + per_b]
            imag = value[q * 2 * per_b + per_b : (q + 1) * 2 * per_b]
            extra = real[:, 128:] + pltpu.roll(imag[:, 128:], 64, 1)
            for n in range(narrow):
                base = ((place * pair + q) * narrow + n) * block
                take = slice(n * per_kt, (n + 1) * per_kt)
                outgoing[base : base + per_kt, :] = real[take, :128]
                outgoing[base + per_kt : base + 2 * per_kt, :] = imag[take, :128]
                outgoing[base + 2 * per_kt : base + 3 * per_kt, :] = extra[take]
                outgoing[base + 3 * per_kt : base + block, :] = jnp.zeros(
                    (block - 3 * per_kt, 128), jnp.float32
                )
        for q in range(pair):
            x = lax.rem(my_x + q, pair)
            for k in range(narrow):
                w, n = group * pair + x, lax.rem(my_n + k, narrow)
                index = (step * pair + q) * narrow + k
                held = pl.ds(
                    pl.multiple_of(((place * pair + x) * narrow + n) * block, 8), 3 * per_kt
                )
                if index == 0:
                    own = pltpu.make_async_copy(outgoing.at[held], arrived.at[mine], own_sem)
                    own.start()
                    continue
                copy = pltpu.make_async_remote_copy(
                    src_ref=outgoing.at[held],
                    dst_ref=arrived.at[mine],
                    send_sem=far_send.at[index],
                    recv_sem=far_recv.at[index],
                    device_id=(w, n),
                    device_id_type=MESH,
                )
                copy.start()
                copies.append(copy)
    own.wait()
    loads[4].wait()
    for step in range(groups):
        for q in range(pair):
            for k in range(narrow):
                index = (step * pair + q) * narrow + k
                if index == 0:
                    continue
                w = lax.rem(my_z + groups - step, groups) * pair + lax.rem(my_x + q, pair)
                n = lax.rem(my_n + narrow - k, narrow)
                pltpu.make_async_remote_copy(
                    src_ref=outgoing.at[pl.ds(0, 3 * per_kt)],
                    dst_ref=arrived.at[span(w, n)],
                    send_sem=far_send.at[index],
                    recv_sem=far_recv.at[index],
                    device_id=(w, n),
                    device_id_type=MESH,
                ).wait_recv()

    third = (third_ref[0], third_ref[1])
    devices = wide * narrow
    momenta = third_ref.shape[1] // 2
    start = lax.broadcasted_iota(jnp.int32, (devices, 128), 1) < over
    for kt in range(0, per_kt, 2):
        columns = []
        for m in range(2):
            real, imag, extra = [
                arrived[pl.ds(part * per_kt + kt + m, devices, stride=block), :]
                for part in range(3)
            ]
            real_one = jnp.where(start, pltpu.roll(real, over, 1), extra)
            imag_one = jnp.where(start, pltpu.roll(imag, over, 1), pltpu.roll(extra, 64, 1))
            columns.append(jnp.concatenate([real, imag, real_one, imag_one], axis=0))
        value = dot3(third, halves(jnp.concatenate(columns, axis=1)), ((1,), (0,)))
        for m in range(2):
            whole = value[:, 128 * m : 128 * (m + 1)].T[:used]
            out_ref[0, :, kt + m] = whole[:, :momenta].reshape(COMPS, ROWS, momenta)
            out_ref[1, :, kt + m] = whole[:, momenta:].reshape(COMPS, ROWS, momenta)
    for copy in copies:
        copy.wait_send()


def message_rows(per_kt):
    return -(-3 * per_kt // 8) * 8


def fused_body(wide, narrow, links, gauge):
    slab_x = gauge.shape[1]
    tables = make_tables(wide, narrow, slab_x)
    devices = wide * narrow
    per_kt = LT // narrow
    block = message_rows(per_kt)
    faces = 4 * HALF_SWEEPS + 2
    vmem = pl.BlockSpec(memory_space=pltpu.VMEM)
    operands = [
        links.reshape(4 * 4 * slab_x * 24, 128),
        gauge.reshape(4 * slab_x * 24, 128),
        *[jnp.asarray(table) for table in tables],
    ]
    spectrum, field = pl.pallas_call(
        lambda *refs: fused(wide, narrow, *refs),
        out_shape=(
            jax.ShapeDtypeStruct((2, COMPS, per_kt, ROWS, wide * slab_x * narrow), jnp.float32),
            jax.ShapeDtypeStruct((4 * slab_x * 24, 128), jnp.float32),
        ),
        in_specs=[pl.BlockSpec(memory_space=pl.ANY)] * len(operands),
        out_specs=(vmem, vmem),
        scratch_shapes=[
            *[pltpu.VMEM(value.shape, value.dtype) for value in operands],
            pltpu.VMEM((faces, 4, ROWS, LANES), jnp.float32),
            pltpu.VMEM((faces, 4, ROWS, LANES), jnp.float32),
            pltpu.VMEM((2, COMPS * ROWS, LANES), jnp.float32),
            pltpu.VMEM((devices * block, 128), jnp.float32),
            pltpu.VMEM((devices * block, 128), jnp.float32),
            pltpu.SemaphoreType.DMA((len(operands),)),
            pltpu.SemaphoreType.DMA((faces,)),
            pltpu.SemaphoreType.DMA((faces,)),
            pltpu.SemaphoreType.DMA((devices,)),
            pltpu.SemaphoreType.DMA((devices,)),
            pltpu.SemaphoreType.DMA,
        ],
        compiler_params=pltpu.CompilerParams(
            collective_id=0, has_side_effects=True, vmem_limit_bytes=VMEM_MIB * 1024 * 1024
        ),
    )(*operands)
    spectrum = jnp.transpose(spectrum, (0, 1, 3, 2, 4))
    return spectrum, field.reshape(gauge.shape)


def solution(mesh):
    in_specs = (P(None, None, "wide", "narrow", None), P(None, "wide", "narrow", None))
    out_specs = (P(None, None, "wide", "narrow", None), P(None, "wide", "narrow", None))
    wide, narrow = mesh.shape["wide"], mesh.shape["narrow"]

    def per_device(links, gauge):
        slab_x, slab_z = gauge.shape[1:3]
        fits = slab_x == 2 and slab_z == 1 and wide * ROWS == LY and wide * narrow * 4 == 128
        if fits:
            return fused_body(wide, narrow, links, gauge)
        return body(links, gauge)

    return jax.shard_map(
        per_device, mesh=mesh, in_specs=in_specs, out_specs=out_specs, check_vma=False
    )
```
